512 devices in a mesh: gx: 8 (over z), gy: 8 (over y), gz: 8 (over x, core).
Axes of the slice: x: 4, y: 8, z: 8, core: 2. Of those that a mesh axis runs over, the one named last changes fastest.
Arguments:
- electric: float32 [3, 64, 128, 1024], P(None, 'gx', 'gy', 'gz'), may hold values from -6 to 6
- electric_prev: float32 [3, 64, 128, 1024], P(None, 'gx', 'gy', 'gz'), may hold values from -6 to 6
- courant: float32 [64, 128, 1024], P('gx', 'gy', 'gz'), may hold values from 0.05 to 0.25
- port_cell: int32 [131072], P(('gx', 'gy', 'gz')), may hold values from 0 to 16383
- port_route: int32 [131072, 1], P(('gx', 'gy', 'gz')), may hold values from 0 to 63; in each aligned block of 256 rows (0 to 255, 256 to 511, ...) at most 8 rows name the same one
- port_group: int32 [131072], P(('gx', 'gy', 'gz')), may hold values from 0 to 7
- port_gain: float32 [131072], P(('gx', 'gy', 'gz')), may hold values from 0.5 to 2
- port_drive: float32 [131072], P(('gx', 'gy', 'gz')), may hold values from 0.3 to 3
- port_bias: float32 [131072], P(('gx', 'gy', 'gz')), may hold values from -5 to 5
- port_couple: float32 [131072], P(('gx', 'gy', 'gz')), may hold values from 0.02 to 0.08
Outputs:
- electric_next: float32 [3, 64, 128, 1024], P(None, 'gx', 'gy', 'gz')
- electric_last: float32 [3, 64, 128, 1024], P(None, 'gx', 'gy', 'gz')
- port_current: float32 [131072], P(('gx', 'gy', 'gz'))
The draws below stay inside these ranges and needn't reach their ends.
Inputs may be any that keep to these rules, and one draw needn't show every extreme that they name: Of the ports of one device, at most 8 have the same port_route, and in every draw some device has exactly 8 ports of one port_route.
All inputs are finite; a program needn't handle non-finite values.
Results may differ from the reference program's by a relative error of at most 0.00015.
Values sent between devices are 32-bit elements; how exact they have to be, the bound alone decides.
A program may use at most 64 MiB of HBM per device.

```python
import math
import jax
import jax.numpy as jnp
import numpy as np

CX = 8
CY = 16
CZ = 128
PORTS_DEV = 256
SUB = 4
ITERS = 3
GROUPS = 8
CAP = 8
NX = 64
NY = 128
NZ = 1024
PORTS = 131072
N_GX = 8
N_GY = 8
N_GZ = 8


def plant(entries, key, least, top_value):
    place = [jax.random.randint(jax.random.fold_in(key, axis), (), 0, length) for axis, length in enumerate(entries.shape)]
    longest = entries.shape.index(max(entries.shape))
    beside = place[:longest] + [(place[longest] + 1) % entries.shape[longest]] + place[longest + 1:]
    return entries.at[tuple(place)].set(least).at[tuple(beside)].set(top_value)


def levels(stream_key, extent, cuts, low, largest):
    def one(position, blocks):
        draws = jax.random.uniform(jax.random.fold_in(jax.random.fold_in(stream_key, 6), position), (blocks,), jnp.float32, low / len(cuts), largest / len(cuts))
        return jnp.repeat(jnp.exp(draws), extent[position] // blocks).reshape((-1,) + (1,) * (len(extent) - position - 1))

    loudness = one(*cuts[0])
    for cut in cuts[1:]:
        loudness = loudness * one(*cut)
    return loudness


def shared_out(key, own, number, rows, number_of, top, reach, skew):
    sequence = jax.random.permutation(key, number_of)
    crowded, ordinary = portions_of(number_of, rows * top, reach, skew, True), portions_of(number_of, rows * top, reach, skew, False)
    places = jnp.arange(number_of)

    def named(lengths, rotation):
        used = int((lengths > 0).sum())
        fixed = max(1, used // 4)
        shifted = fixed + (places - fixed + rotation * (used - fixed)) % max(1, number_of - fixed)
        return jnp.zeros((number_of,), jnp.int32).at[sequence[jnp.where(places < fixed, places, shifted)]].set(jnp.asarray(lengths, jnp.int32))

    lengths = jnp.where(number % 4 == 0, named(crowded, number // 4), named(ordinary, number - number // 4 - 1))
    mixed = jax.random.permutation(jax.random.fold_in(own, 3), number_of)
    donor, receiver = mixed[0:number_of // 2 * 2:2], mixed[1:number_of // 2 * 2:2]
    slack = jnp.minimum(lengths[donor] - 1, reach - lengths[receiver]) // 2
    slack = jnp.where((donor == sequence[0]) | (receiver == sequence[0]) | (lengths[receiver] == 0), 0, jnp.maximum(slack, 0))
    shifted = jax.random.randint(jax.random.fold_in(own, 4), (number_of // 2,), 0, 1 << 20) % (slack + 1)
    lengths = lengths.at[donor].add(-shifted).at[receiver].add(shifted)
    labels = jnp.searchsorted(jnp.cumsum(lengths), jnp.arange(rows * top), side="right").astype(jnp.int32)
    listing = labels.reshape(top, rows).T
    listing = listing[jax.random.permutation(jax.random.fold_in(own, 1), rows)]
    rotation = jax.random.randint(jax.random.fold_in(own, 2), (rows, 1), 0, top)
    return jnp.take_along_axis(listing, (jnp.arange(top)[None, :] + rotation) % top, axis=1)


def portions_of(amount, total, limit, slope, full):
    weights = [(1 << 20) // math.isqrt(standing ** slope) + 1 for standing in range(1, amount + 1)]
    largest = limit if full else min(limit, max(-(-total // amount), total * weights[0] // sum(weights)))
    least = 1 if total - largest >= amount - 1 else 0
    given, rest = [largest] + [least] * (amount - 1), total - largest - least * (amount - 1)
    while rest > 0:
        movable = [i for i in range(1, amount) if given[i] < largest] or [i for i in range(1, amount) if given[i] < limit]
        pool, budget = sum([weights[i] for i in movable]), rest
        for i in movable:
            extra = min(limit - given[i], max(1, budget * weights[i] // pool), rest)
            given[i] = given[i] + extra
            rest = rest - extra
    return np.array(given)


def gaussian(key, dims, scale, bound, split=(), kind=jnp.bfloat16):
    values = jax.random.normal(key, dims, jnp.float32) * scale
    if len(split) > 0:
        values = levels(key, dims, split, -0.22, 0.18) * values
    return jnp.clip(values, min=-bound, max=bound).astype(kind)


def setup_inputs(seed: int = 0) -> dict:
    splits = jax.random.split(jax.random.key(seed), 11)
    electric = gaussian(splits[0], (3, NX, NY, NZ), 1.0, 6.0, ((1, 8), (2, 8), (3, 8)), jnp.float32)
    electric_prev = gaussian(splits[1], (3, NX, NY, NZ), 1.0, 6.0, ((1, 8), (2, 8), (3, 8)), jnp.float32)
    courant = jnp.clip(jnp.exp(math.log(0.25) - 1.609438 * jax.random.uniform(splits[2], (NX, NY, NZ), jnp.float32) ** levels(splits[2], (NX, NY, NZ), ((0, 8), (1, 8), (2, 8)), -0.2, 0.2)), 0.05, 0.25)
    port_cell = plant(jax.random.randint(splits[3], (PORTS,), 0, CX * CY * CZ), jax.random.fold_in(splits[3], 1), 0, (CX * CY * CZ) - 1).astype(jnp.int32)
    port_route_keys = jax.random.split(jax.random.fold_in(splits[4], 1), PORTS // PORTS_DEV)
    port_route_turns = jax.random.permutation(jax.random.fold_in(splits[4], 3), PORTS // PORTS_DEV)
    port_route = jax.vmap(lambda own, number: shared_out(jax.random.fold_in(splits[4], 2), own, number, PORTS_DEV, N_GY * N_GZ, 1, CAP, 2))(port_route_keys, port_route_turns).reshape((PORTS, 1))
    port_group = plant(jax.random.randint(splits[5], (PORTS,), 0, GROUPS), jax.random.fold_in(splits[5], 1), 0, GROUPS - 1).astype(jnp.int32)
    port_gain = jnp.clip(jnp.exp(math.log(2.0) - 1.3862944 * jax.random.uniform(splits[6], (PORTS,), jnp.float32) ** levels(splits[6], (PORTS,), ((0, 512),), -0.2, 0.2)), 0.5, 2.0)
    port_drive = jnp.clip(jnp.exp(math.log(3.0) - 2.3025851 * jax.random.uniform(splits[7], (PORTS,), jnp.float32) ** levels(splits[7], (PORTS,), ((0, 512),), -0.2, 0.2)), 0.3, 3.0)
    port_bias = gaussian(splits[8], (PORTS,), 1.0, 5.0, ((0, 512),), jnp.float32)
    port_couple = jnp.clip(jnp.exp(math.log(0.08) - 1.3862944 * jax.random.uniform(splits[9], (PORTS,), jnp.float32) ** levels(splits[9], (PORTS,), ((0, 512),), -0.2, 0.2)), 0.02, 0.08)
    return {"electric": electric, "electric_prev": electric_prev, "courant": courant, "port_cell": port_cell, "port_route": port_route, "port_group": port_group, "port_gain": port_gain, "port_drive": port_drive, "port_bias": port_bias, "port_couple": port_couple}


def curl_curl(padded):
    field_x, field_y, field_z = padded[0], padded[1], padded[2]
    curl_x = (field_z[:-1, 1:, :-1] - field_z[:-1, :-1, :-1]) - (field_y[:-1, :-1, 1:] - field_y[:-1, :-1, :-1])
    curl_y = (field_x[:-1, :-1, 1:] - field_x[:-1, :-1, :-1]) - (field_z[1:, :-1, :-1] - field_z[:-1, :-1, :-1])
    curl_z = (field_y[1:, :-1, :-1] - field_y[:-1, :-1, :-1]) - (field_x[:-1, 1:, :-1] - field_x[:-1, :-1, :-1])
    back_x = (curl_z[1:, 1:, 1:] - curl_z[1:, :-1, 1:]) - (curl_y[1:, 1:, 1:] - curl_y[1:, 1:, :-1])
    back_y = (curl_x[1:, 1:, 1:] - curl_x[1:, 1:, :-1]) - (curl_z[1:, 1:, 1:] - curl_z[:-1, 1:, 1:])
    back_z = (curl_y[1:, 1:, 1:] - curl_y[:-1, 1:, 1:]) - (curl_x[1:, 1:, 1:] - curl_x[1:, :-1, 1:])
    return jnp.stack([back_x, back_y, back_z])


def reference(electric, electric_prev, courant, port_cell, port_route, port_group, port_gain, port_drive, port_bias, port_couple):
    present, previous = electric, electric_prev
    for substep in range(SUB):
        padded = jnp.pad(present, ((0, 0), (1, 1), (1, 1), (1, 1)))
        updated = 2.0 * present - previous - courant[None] * curl_curl(padded)
        previous, present = present, updated
    peer_count = N_GY * N_GZ
    port_index = jnp.arange(PORTS, dtype=jnp.int32)
    device_id = port_index // PORTS_DEV
    plane_x = device_id // peer_count
    row_y = (device_id // N_GZ) % N_GY
    row_z = device_id % N_GZ
    local_x = port_cell // (CY * CZ)
    local_y = (port_cell // CZ) % CY
    local_z = port_cell % CZ
    global_cell = ((plane_x * CX + local_x) * NY + (row_y * CY + local_y)) * NZ + row_z * CZ + local_z
    ez_flat = present[2].reshape(-1)
    sample = ez_flat[global_cell]
    segment = (plane_x * peer_count + port_route[:, 0]) * GROUPS + port_group
    node_volt = sample
    for iterate in range(ITERS):
        squash = jnp.tanh(node_volt)
        totals = jax.ops.segment_sum(squash, segment, num_segments=N_GX * peer_count * GROUPS)
        shared = totals[segment]
        resid = (1.0 + port_gain) * node_volt - sample - port_bias + port_drive * squash + port_couple * shared
        slope_diag = 1.0 + port_gain + (port_drive + port_couple) * (1.0 - squash * squash)
        node_volt = node_volt - resid / slope_diag
    current = port_gain * (node_volt - sample)
    ez_next = ez_flat.at[global_cell].add(current).reshape(NX, NY, NZ)
    electric_next = present.at[2].set(ez_next)
    return electric_next, previous, current
```

```python
import jax
import jax.numpy as jnp
from jax import lax
from jax.experimental import pallas as pl
from jax.experimental.pallas import tpu as pltpu
from jax.sharding import PartitionSpec as P

MESH = pl.DeviceIdType.MESH
F32 = jnp.float32
BF16 = jnp.bfloat16
N = 8
W = 4
CX, CY, CZ = 8, 16, 128
EX, EY = CX + 2 * W, CY + 2 * W
PORTS = 256
GROUPS = 8
NPAR = 5


def pieces(value):
    high = value.astype(BF16).astype(F32)
    rest = value - high
    mid = rest.astype(BF16).astype(F32)
    return high, mid, rest - mid


def dot_nt(a, b):
    return lax.dot_general(a, b, (((1,), (1,)), ((), ())), preferred_element_type=F32)


def dot_nn(a, b):
    return lax.dot_general(a, b, (((1,), (0,)), ((), ())), preferred_element_type=F32)


def three(dot, value, other):
    rows = value.shape[0]
    out = dot(jnp.concatenate(pieces(value), axis=0).astype(BF16), other)
    return (out[:rows] + out[rows : 2 * rows]) + out[2 * rows :]


def up_z(main, halo, lane):
    rm, rh = pltpu.roll(main, CZ - 1, 1), pltpu.roll(halo, CZ - 1, 1)
    return jnp.where(lane == CZ - 1, rh, rm), jnp.where(lane == CZ - 1, rm, rh)


def down_z(main, halo, lane):
    rm, rh = pltpu.roll(main, 1, 1), pltpu.roll(halo, 1, 1)
    return jnp.where(lane == 0, rh, rm), jnp.where(lane == 0, rm, rh)


def up_y(v):
    return pltpu.roll(v, EY - 1, 0)


def down_y(v):
    return pltpu.roll(v, 1, 0)


def substep(now, now_h, old, old_h, cou, cou_h, low, high, last):
    lane = lax.broadcasted_iota(jnp.int32, (EY, CZ), 1)

    def curls(x):
        vx, vy, vz = now[0, x], now[1, x], now[2, x]
        vxh, vyh, vzh = now_h[0, x], now_h[1, x], now_h[2, x]
        vxu, vxuh = up_z(vx, vxh, lane)
        gy = (vxu - vx) - (now[2, x + 1] - vz)
        gyh = (vxuh - vxh) - (now_h[2, x + 1] - vzh)
        gz = (now[1, x + 1] - vy) - (up_y(vx) - vx)
        gzh = (now_h[1, x + 1] - vyh) - (up_y(vxh) - vxh)
        return gy, gyh, gz, gzh

    def body(x, carry):
        gyp, gyph, gzp, gzph = carry
        vx, vy, vz = now[0, x], now[1, x], now[2, x]
        vxh, vyh, vzh = now_h[0, x], now_h[1, x], now_h[2, x]
        gy, gyh, gz, gzh = curls(x)
        vyu, vyuh = up_z(vy, vyh, lane)
        gx = (up_y(vz) - vz) - (vyu - vy)
        gxh = (up_y(vzh) - vzh) - (vyuh - vyh)
        gxd, gxdh = down_z(gx, gxh, lane)
        gyd, gydh = down_z(gy, gyh, lane)
        c = cou[x]
        kx = (gz - down_y(gz)) - (gy - gyd)
        ky = (gx - gxd) - (gz - gzp)
        kz = (gy - gyp) - (gx - down_y(gx))
        old[0, x] = 2.0 * vx - old[0, x] - c * kx
        old[1, x] = 2.0 * vy - old[1, x] - c * ky
        old[2, x] = 2.0 * vz - old[2, x] - c * kz
        if not last:
            ch = cou_h[x]
            kxh = (gzh - down_y(gzh)) - (gyh - gydh)
            kyh = (gxh - gxdh) - (gzh - gzph)
            kzh = (gyh - gyph) - (gxh - down_y(gxh))
            old_h[0, x] = 2.0 * vxh - old_h[0, x] - ch * kxh
            old_h[1, x] = 2.0 * vyh - old_h[1, x] - ch * kyh
            old_h[2, x] = 2.0 * vzh - old_h[2, x] - ch * kzh
        return gy, gyh, gz, gzh

    lax.fori_loop(low, high, body, curls(low - 1))


def kernel(
    e_ref,
    ep_ref,
    co_ref,
    cell_ref,
    route_ref,
    group_ref,
    gain_ref,
    drive_ref,
    bias_ref,
    couple_ref,
    next_ref,
    last_ref,
    cur_ref,
    own,
    a,
    ah,
    b,
    bh,
    c,
    ch,
    pz,
    px,
    py,
    pc,
    qz,
    qx,
    qy,
    qc,
    iport,
    fport,
    ownpar,
    ownsam,
    par,
    sam,
    node,
    finz,
    curv,
    drain,
    lsem,
    hsend,
    hrecv,
    ysend,
    yrecv,
    xsend,
    xrecv,
    tsem,
    ssend,
    srecv,
):
    gx, gy, gz = lax.axis_index("gx"), lax.axis_index("gy"), lax.axis_index("gz")
    me = gz * N + gy

    def near(dx, dy, dz):
        return (lax.rem(gx + N + dx, N), lax.rem(gy + N + dy, N), lax.rem(gz + N + dz, N))

    barrier = pltpu.get_barrier_semaphore()

    for dx in (-1, 1):
        for dy in (-1, 0, 1):
            for dz in (-1, 0, 1):
                pl.semaphore_signal(barrier, inc=1, device_id=near(dx, dy, dz), device_id_type=MESH)

    def greet(k, _):
        t = lax.rem(me + k, N * N)
        pl.semaphore_signal(
            barrier, inc=1, device_id=(gx, lax.rem(t, N), t // N), device_id_type=MESH
        )
        return 0

    lax.fori_loop(1, N * N, greet, 0)

    inner = (pl.ds(W, CX), pl.ds(W, CY))
    local = [
        (e_ref, own.at[0:3]),
        (ep_ref, own.at[3:6]),
        (co_ref, own.at[6]),
        (cell_ref, iport.at[0]),
        (route_ref, iport.at[1]),
        (group_ref, iport.at[2]),
        (gain_ref, fport.at[0]),
        (drive_ref, fport.at[1]),
        (bias_ref, fport.at[2]),
        (couple_ref, fport.at[3]),
        (e_ref, a.at[:, inner[0], inner[1]]),
        (ep_ref, b.at[:, inner[0], inner[1]]),
        (co_ref, c.at[inner[0], inner[1]]),
    ]
    local = [pltpu.make_async_copy(s, d, lsem.at[i]) for i, (s, d) in enumerate(local)]
    for copy in local:
        copy.start()
    for copy in local[:3]:
        copy.wait()

    lane = lax.broadcasted_iota(jnp.int32, (CZ, CZ), 1)
    packed = jnp.zeros((CZ, CZ), F32)
    for f in range(7):
        rolled = pltpu.roll(own[f].reshape(CZ, CZ), W + 8 * f, 1)
        packed = jnp.where(lane // 8 == f, rolled, packed)
    packed = packed.T
    lane8 = lax.broadcasted_iota(jnp.int32, (8, CZ), 1)
    slot = lane8 % CY // W
    rows = [packed[8 * f : 8 * f + 8] for f in range(7)]
    for f in range(7):
        pz[f] = rows[f]

    def turn(v, shift):
        shift = shift % CZ
        return v if shift == 0 else pltpu.roll(v, shift, 1)

    def quarters(group, top):
        out = turn(group[0], -12 if top else 0)
        for j in range(1, len(group)):
            out = jnp.where(slot == j, turn(group[j], 4 * j - (12 if top else 0)), out)
        return out

    halves = []
    for top in (0, 1):
        tiles = []
        for j in range(4):
            if j == 3:
                tile = turn(rows[3], 64 * top)
            elif top:
                tile = jnp.where(lane8 < 64, turn(rows[j], 64), rows[j + 4])
            else:
                tile = jnp.where(lane8 < 64, rows[j], turn(rows[j + 4], 64))
            px[top, j] = tile
            tiles.append(tile)
        halves.append(tiles)
    for top in (0, 1):
        py[top, 0] = quarters(rows[0:4], top)
        py[top, 1] = quarters(rows[4:7], top)
        for xt in (0, 1):
            pc[xt, top] = quarters(halves[xt], top)

    for copy in local[3:]:
        copy.wait()
    route = iport[1]
    at64 = lax.broadcasted_iota(jnp.int32, (64, PORTS), 0) == route
    earlier = lax.broadcasted_iota(jnp.int32, (PORTS, PORTS), 0) < lax.broadcasted_iota(
        jnp.int32, (PORTS, PORTS), 1
    )
    count = dot_nn(
        jnp.where(at64, 1.0, 0.0).astype(BF16), jnp.where(earlier, 1.0, 0.0).astype(BF16)
    )
    rank = jnp.sum(jnp.where(at64, count, 0.0), axis=0, keepdims=True).astype(jnp.int32)
    slot_lane = route + 64 * (rank % 2)
    slot_row = rank // 2
    iota128 = lax.broadcasted_iota(jnp.int32, (CZ, PORTS), 0)
    to_lane = jnp.where(iota128 == slot_lane, 1.0, 0.0).astype(BF16)
    iota8 = lax.broadcasted_iota(jnp.int32, (8, PORTS), 0)
    in_row = iota8 % 4 == slot_row
    values = [fport[0], fport[1], fport[2], fport[3], iport[2].astype(F32) + 1.0]
    stacked = jnp.concatenate(
        [
            jnp.where(in_row, jnp.where(iota8 < 4, values[2 * i], values[min(2 * i + 1, 4)]), 0.0)
            for i in range(3)
        ],
        axis=0,
    )
    slots = three(dot_nt, stacked, to_lane)
    for i in range(NPAR):
        ownpar[i] = slots[4 * i : 4 * i + 4]
    cell = iport[0]
    row_hot = iota128 == cell // CZ
    z_hot = iota128 == cell % CZ

    pl.semaphore_wait(barrier, N * N - 1 + 18)

    def span(d, width, size):
        if d == 0:
            return pl.ds(0, size), pl.ds(W, size)
        if d > 0:
            return pl.ds(size - width, width), pl.ds(W - width, width)
        return pl.ds(0, width), pl.ds(W + size, width)

    halo = []

    def send(src, dst, d):
        i = len(halo)
        copy = pltpu.make_async_remote_copy(
            src_ref=src,
            dst_ref=dst,
            send_sem=hsend.at[i],
            recv_sem=hrecv.at[i],
            device_id=near(*d),
            device_id_type=MESH,
        )
        copy.start()
        halo.append(copy)

    flat = [(1, 0), (-1, 0), (1, 1), (1, -1), (-1, 1), (-1, -1), (0, 1), (0, -1)]
    for dx, dy in flat:
        sx4, tx4 = span(dx, W, CX)
        sy4, ty4 = span(dy, W, CY)
        sx3, tx3 = span(dx, W - 1, CX)
        sy3, ty3 = span(dy, W - 1, CY)
        send(own.at[0:3, sx4, sy4], a.at[:, tx4, ty4], (dx, dy, 0))
        send(own.at[3:6, sx3, sy3], b.at[:, tx3, ty3], (dx, dy, 0))
        send(own.at[6, sx3, sy3], c.at[tx3, ty3], (dx, dy, 0))
    n_flat = len(halo)
    for dz in (1, -1):
        part = pl.ds(0, W) if dz > 0 else pl.ds(W, W)
        send(pz.at[:, part], qz.at[:, part], (0, 0, dz))
        for d in (1, -1):
            mine, theirs = (1, 0) if d > 0 else (0, 1)
            send(px.at[mine, :, part], qx.at[theirs, :, part], (d, 0, dz))
            send(py.at[mine, :, part], qy.at[theirs, :, part], (0, d, dz))
            for dy in (1, -1):
                mine_y, theirs_y = (1, 0) if dy > 0 else (0, 1)
                send(pc.at[mine, mine_y, part], qc.at[theirs, theirs_y, part], (d, dy, dz))

    half = pl.ds(4 * lax.rem(gy, 2), 4)
    spread_y = []
    for k in range(1, N):
        copy = pltpu.make_async_remote_copy(
            src_ref=ownpar,
            dst_ref=par.at[gz, gy // 2, :, half],
            send_sem=ysend.at[k - 1],
            recv_sem=yrecv.at[k - 1],
            device_id=(gx, lax.rem(gy + k, N), gz),
            device_id_type=MESH,
        )
        copy.start()
        spread_y.append(copy)
    own_par = pltpu.make_async_copy(ownpar, par.at[gz, gy // 2, :, half], lsem.at[0])
    own_par.start()

    for copy in halo[n_flat:]:
        copy.wait_recv()
    low_ok = jnp.where(gz > 0, 1, 0)
    high_ok = jnp.where(gz < N - 1, 1, 0)
    keep = jnp.where(lane < CZ // 2, high_ok, low_ok) == 1

    def unpack(tiles, store):
        block = jnp.concatenate(tiles + [jnp.zeros((CZ - 56, CZ), F32)], axis=0).T
        for f in range(7):
            value = jnp.where(keep, pltpu.roll(block, (CZ - 8 * f - W) % CZ, 1), 0.0)
            ref = (ah, bh, ch)[f // 3]
            store(ref if f == 6 else ref.at[f % 3], value)

    def store_own(ref, value):
        ref[W : W + CX, W : W + CY] = value.reshape(CX, CY, CZ)

    def store_x(ref, value):
        value = value.reshape(CX, CY, CZ)
        ref[0:W, W : W + CY] = value[:W]
        ref[W + CX :, W : W + CY] = value[W:]

    def store_y(ref, value):
        value = value.reshape(CX, 4, W, CZ)
        ref[W : W + CX, 0:W] = value[:, 0]
        ref[W : W + CX, W + CY :] = value[:, 1]
        ref[0:W, 0:W] = value[:W, 2]
        ref[W + CX :, 0:W] = value[W:, 2]
        ref[0:W, W + CY :] = value[:W, 3]
        ref[W + CX :, W + CY :] = value[W:, 3]

    unpack([qz[f] for f in range(7)], store_own)
    tiles = []
    for f in range(7):
        h, j = f // 4, f % 4
        if h == 0:
            tiles.append(jnp.where(lane8 < 64, qx[0, j], pltpu.roll(qx[1, j], 64, 1)))
        else:
            tiles.append(jnp.where(lane8 < 64, pltpu.roll(qx[0, j], 64, 1), qx[1, j]))
    unpack(tiles, store_x)
    tiles = []
    for f in range(7):
        h, j = f // 4, f % 4
        tile = jnp.where(slot == 0, turn(qy[0, h], -4 * j), turn(qy[1, h], 4 - 4 * j))
        for s in (0, 1):
            shift = 8 + 4 * s - 4 * j - 64 * h
            corner = jnp.where(lane8 < 64, turn(qc[0, s], shift), turn(qc[1, s], shift + 64))
            tile = jnp.where(slot == 2 + s, corner, tile)
        tiles.append(tile)
    unpack(tiles, store_y)

    own_par.wait()
    for copy in spread_y:
        copy.wait_recv()
    spread_x = []
    for k in range(1, 4):
        copy = pltpu.make_async_remote_copy(
            src_ref=par.at[gz],
            dst_ref=par.at[gz],
            send_sem=xsend.at[k - 1],
            recv_sem=xrecv.at[k - 1],
            device_id=(gx, gy, lax.rem(gz + 2 * k, N)),
            device_id_type=MESH,
        )
        copy.start()
        spread_x.append(copy)

    for copy in halo[:n_flat]:
        copy.wait_recv()

    def clear(xs, ys):
        for ref in (a, ah, b, bh):
            ref[:, xs, ys] = jnp.zeros_like(ref[:, xs, ys])
        for ref in (c, ch):
            ref[xs, ys] = jnp.zeros_like(ref[xs, ys])

    @pl.when(gx == 0)
    def _():
        clear(slice(0, W), slice(0, EY))

    @pl.when(gx == N - 1)
    def _():
        clear(slice(W + CX, EX), slice(0, EY))

    @pl.when(gy == 0)
    def _():
        clear(slice(0, EX), slice(0, W))

    @pl.when(gy == N - 1)
    def _():
        clear(slice(0, EX), slice(W + CY, EY))

    substep(a, ah, b, bh, c, ch, 1, EX - 1, False)
    substep(b, bh, a, ah, c, ch, 2, EX - 2, False)
    substep(a, ah, b, bh, c, ch, 3, EX - 3, False)
    out_last = pltpu.make_async_copy(b.at[:, inner[0], inner[1]], last_ref, lsem.at[1])
    out_last.start()
    substep(b, bh, a, ah, c, ch, 4, EX - 4, True)
    out_next = pltpu.make_async_copy(
        a.at[0:2, inner[0], inner[1]], next_ref.at[0:2], lsem.at[2]
    )
    out_next.start()

    ez = a[2, W : W + CX, W : W + CY].reshape(CZ, CZ)
    row_one = jnp.where(row_hot, 1.0, 0.0).astype(BF16)
    picked = three(dot_nn, ez.T, row_one)
    sample = jnp.sum(jnp.where(z_hot, picked, 0.0), axis=0, keepdims=True)
    sample8 = three(dot_nt, jnp.where(in_row, sample, 0.0), to_lane)
    ownsam[...] = sample8[0:4]
    for k in range(1, N * N):
        t = lax.rem(me + k, N * N)
        pltpu.make_async_remote_copy(
            src_ref=ownsam,
            dst_ref=sam.at[gz, gy // 2, half],
            send_sem=ssend,
            recv_sem=srecv,
            device_id=(gx, lax.rem(t, N), t // N),
            device_id_type=MESH,
        ).start()
    own_sam = pltpu.make_async_copy(ownsam, sam.at[gz, gy // 2, half], lsem.at[0])
    own_sam.start()

    for copy in spread_x:
        copy.wait_recv()
    core = lax.rem(gz, 2)
    twins = []
    for i in range(4):
        copy = pltpu.make_async_remote_copy(
            src_ref=par.at[2 * i + core],
            dst_ref=par.at[2 * i + core],
            send_sem=tsem.at[0, i],
            recv_sem=tsem.at[1, i],
            device_id=(gx, gy, gz + 1 - 2 * core),
            device_id_type=MESH,
        )
        copy.start()
        twins.append(copy)
    for copy in twins:
        copy.wait_recv()
    own_sam.wait()
    pltpu.make_async_copy(drain, drain, srecv).wait()

    sub = lax.broadcasted_iota(jnp.int32, (8, CZ), 0)

    def totals(first):
        def add(i, acc):
            for j in range(N // 2):
                volt = sam[i, j] if first else node[i, j]
                s = jnp.tanh(volt)
                grp = par[i, j, 4]
                acc = tuple(
                    acc[g] + jnp.where(grp == float(g + 1), s, 0.0) for g in range(GROUPS)
                )
            return acc

        acc = lax.fori_loop(0, N, add, tuple(jnp.zeros((8, CZ), F32) for _ in range(GROUPS)))
        total = jnp.zeros((8, CZ), F32)
        for g in range(GROUPS):
            total = jnp.where(sub == g, jnp.sum(acc[g], axis=0, keepdims=True), total)
        return total + pltpu.roll(total, 64, 1)

    def newton(volt, sample, gain, drive, bias, couple, grp, total):
        s = jnp.tanh(volt)
        shared = jnp.zeros_like(volt)
        for g in range(GROUPS):
            shared = jnp.where(grp == float(g + 1), total[g : g + 1], shared)
        resid = (1.0 + gain) * volt - sample - bias + drive * s + couple * shared
        slope = 1.0 + gain + (drive + couple) * (1.0 - s * s)
        return volt - resid / slope

    mine = sample8
    my = [ownpar[i] for i in range(NPAR)]
    my = [jnp.concatenate([v, v], axis=0) for v in my]
    volt = mine
    for iterate in range(3):
        total = totals(iterate == 0)
        volt = newton(volt, mine, *my, total)
        if iterate < 2:

            def move(i, _):
                for j in range(N // 2):
                    start = sam[i, j]
                    now = start if iterate == 0 else node[i, j]
                    node[i, j] = newton(
                        now, start, *[par[i, j, p] for p in range(NPAR)], total
                    )
                return 0

            lax.fori_loop(0, N, move, 0)
    current = my[0] * (volt - mine)

    spread = three(dot_nn, current, to_lane)
    port = jnp.sum(jnp.where(in_row & (iota8 < 4), spread, 0.0), axis=0, keepdims=True)
    curv[...] = port
    out_cur = pltpu.make_async_copy(curv, cur_ref, lsem.at[3])
    out_cur.start()
    z_one = jnp.where(z_hot, 1.0, 0.0).astype(BF16)
    extra = three(dot_nt, jnp.where(row_hot, port, 0.0), z_one)
    finz[...] = (a[2, W : W + CX, W : W + CY].reshape(CZ, CZ) + extra).reshape(CX, CY, CZ)
    out_z = pltpu.make_async_copy(finz, next_ref.at[2], lsem.at[4])
    out_z.start()
    for copy in (out_last, out_next, out_cur, out_z):
        copy.wait()
    for copy in halo + spread_y + spread_x + twins:
        copy.wait_send()
    pltpu.make_async_copy(drain, drain, ssend).wait()


def on_device(e, ep, co, cell, route, group, gain, drive, bias, couple):
    line = lambda v: v.reshape(1, PORTS)
    any_spec = pl.BlockSpec(memory_space=pl.ANY)
    dma = pltpu.SemaphoreType.DMA
    ext, ext1 = pltpu.VMEM((3, EX, EY, CZ), F32), pltpu.VMEM((EX, EY, CZ), F32)
    electric, last, current = pl.pallas_call(
        kernel,
        out_shape=(
            jax.ShapeDtypeStruct((3, CX, CY, CZ), F32),
            jax.ShapeDtypeStruct((3, CX, CY, CZ), F32),
            jax.ShapeDtypeStruct((1, PORTS), F32),
        ),
        in_specs=[any_spec] * 10,
        out_specs=(any_spec,) * 3,
        scratch_shapes=[
            pltpu.VMEM((7, CX, CY, CZ), F32),
            ext,
            ext,
            ext,
            ext,
            ext1,
            ext1,
            pltpu.VMEM((7, 8, CZ), F32),
            pltpu.VMEM((2, 4, 8, CZ), F32),
            pltpu.VMEM((2, 2, 8, CZ), F32),
            pltpu.VMEM((2, 2, 8, CZ), F32),
            pltpu.VMEM((7, 8, CZ), F32),
            pltpu.VMEM((2, 4, 8, CZ), F32),
            pltpu.VMEM((2, 2, 8, CZ), F32),
            pltpu.VMEM((2, 2, 8, CZ), F32),
            pltpu.VMEM((3, 1, PORTS), jnp.int32),
            pltpu.VMEM((4, 1, PORTS), F32),
            pltpu.VMEM((NPAR, 4, CZ), F32),
            pltpu.VMEM((4, CZ), F32),
            pltpu.VMEM((N, N // 2, NPAR, 8, CZ), F32),
            pltpu.VMEM((N, N // 2, 8, CZ), F32),
            pltpu.VMEM((N, N // 2, 8, CZ), F32),
            pltpu.VMEM((CX, CY, CZ), F32),
            pltpu.VMEM((1, PORTS), F32),
            pltpu.VMEM((N * N - 1, 4, CZ), F32),
            dma((13,)),
            dma((42,)),
            dma((42,)),
            dma((N - 1,)),
            dma((N - 1,)),
            dma((3,)),
            dma((3,)),
            dma((2, 4)),
            dma,
            dma,
        ],
        compiler_params=pltpu.CompilerParams(
            collective_id=0, has_side_effects=True, vmem_limit_bytes=32 * 1024 * 1024
        ),
    )(e, ep, co, line(cell), line(route), line(group), line(gain), line(drive), line(bias), line(couple))
    return electric, last, current.reshape(PORTS)


def solution(mesh):
    field = P(None, "gx", "gy", "gz")
    port = P(("gx", "gy", "gz"))
    placed = (
        field,
        field,
        P("gx", "gy", "gz"),
        port,
        P(("gx", "gy", "gz"), None),
        port,
        port,
        port,
        port,
        port,
    )
    return jax.shard_map(
        on_device,
        mesh=mesh,
        in_specs=placed,
        out_specs=(field, field, port),
        check_vma=False,
    )
```

```python
import jax
import jax.numpy as jnp
from jax import lax
from jax.experimental import pallas as pl
from jax.experimental.pallas import tpu as pltpu
from jax.sharding import PartitionSpec as P

MESH = pl.DeviceIdType.MESH
F32 = jnp.float32
BF16 = jnp.bfloat16
N = 8
W = 4
CX, CY, CZ = 8, 16, 128
EX, EY = CX + 2 * W, CY + 2 * W
PORTS = 256
GROUPS = 8
NPAR = 5


def pieces(value):
    high = value.astype(BF16).astype(F32)
    rest = value - high
    mid = rest.astype(BF16).astype(F32)
    return high, mid, rest - mid


def dot_nt(a, b):
    return lax.dot_general(a, b, (((1,), (1,)), ((), ())), preferred_element_type=F32)


def dot_nn(a, b):
    return lax.dot_general(a, b, (((1,), (0,)), ((), ())), preferred_element_type=F32)


def three(dot, value, other):
    rows = value.shape[0]
    out = dot(jnp.concatenate(pieces(value), axis=0).astype(BF16), other)
    return (out[:rows] + out[rows : 2 * rows]) + out[2 * rows :]


def run(name, phase):
    phase()


def up_z(main, halo, lane):
    rm, rh = pltpu.roll(main, CZ - 1, 1), pltpu.roll(halo, CZ - 1, 1)
    return jnp.where(lane == CZ - 1, rh, rm), jnp.where(lane == CZ - 1, rm, rh)


def down_z(main, halo, lane):
    rm, rh = pltpu.roll(main, 1, 1), pltpu.roll(halo, 1, 1)
    return jnp.where(lane == 0, rh, rm), jnp.where(lane == 0, rm, rh)


def up_y(v):
    return pltpu.roll(v, EY - 1, 0)


def down_y(v):
    return pltpu.roll(v, 1, 0)


def substep(now, now_h, old, old_h, cou, cou_h, low, high, last):
    lane = lax.broadcasted_iota(jnp.int32, (EY, CZ), 1)

    def curls(x):
        vx, vy, vz = now[0, x], now[1, x], now[2, x]
        vxh, vyh, vzh = now_h[0, x], now_h[1, x], now_h[2, x]
        vxu, vxuh = up_z(vx, vxh, lane)
        gy = (vxu - vx) - (now[2, x + 1] - vz)
        gyh = (vxuh - vxh) - (now_h[2, x + 1] - vzh)
        gz = (now[1, x + 1] - vy) - (up_y(vx) - vx)
        gzh = (now_h[1, x + 1] - vyh) - (up_y(vxh) - vxh)
        return gy, gyh, gz, gzh

    def body(x, carry):
        gyp, gyph, gzp, gzph = carry
        vx, vy, vz = now[0, x], now[1, x], now[2, x]
        vxh, vyh, vzh = now_h[0, x], now_h[1, x], now_h[2, x]
        gy, gyh, gz, gzh = curls(x)
        vyu, vyuh = up_z(vy, vyh, lane)
        gx = (up_y(vz) - vz) - (vyu - vy)
        gxh = (up_y(vzh) - vzh) - (vyuh - vyh)
        gxd, gxdh = down_z(gx, gxh, lane)
        gyd, gydh = down_z(gy, gyh, lane)
        c = cou[x]
        kx = (gz - down_y(gz)) - (gy - gyd)
        ky = (gx - gxd) - (gz - gzp)
        kz = (gy - gyp) - (gx - down_y(gx))
        old[0, x] = 2.0 * vx - old[0, x] - c * kx
        old[1, x] = 2.0 * vy - old[1, x] - c * ky
        old[2, x] = 2.0 * vz - old[2, x] - c * kz
        if not last:
            ch = cou_h[x]
            kxh = (gzh - down_y(gzh)) - (gyh - gydh)
            kyh = (gxh - gxdh) - (gzh - gzph)
            kzh = (gyh - gyph) - (gxh - down_y(gxh))
            old_h[0, x] = 2.0 * vxh - old_h[0, x] - ch * kxh
            old_h[1, x] = 2.0 * vyh - old_h[1, x] - ch * kyh
            old_h[2, x] = 2.0 * vzh - old_h[2, x] - ch * kzh
        return gy, gyh, gz, gzh

    carry = curls(low - 1)
    for x in range(low, high):
        carry = body(x, carry)


def kernel(
    e_ref,
    ep_ref,
    co_ref,
    cell_ref,
    route_ref,
    group_ref,
    gain_ref,
    drive_ref,
    bias_ref,
    couple_ref,
    next_ref,
    last_ref,
    cur_ref,
    own,
    a,
    ah,
    b,
    bh,
    c,
    ch,
    pz,
    px,
    py,
    pc,
    qz,
    qx,
    qy,
    qc,
    iport,
    fport,
    ownpar,
    ownsam,
    par,
    sam,
    node,
    drain,
    rowm,
    lanem,
    cellm,
    zm,
    sample8,
    current8,
    lsem,
    hsend,
    hrecv,
    ysend,
    yrecv,
    xsend,
    xrecv,
    tsem,
    ssend,
    srecv,
    plane,
):
    gx, gy, gz = lax.axis_index("gx"), lax.axis_index("gy"), lax.axis_index("gz")
    me = gz * N + gy

    def near(dx, dy, dz):
        return (lax.rem(gx + N + dx, N), lax.rem(gy + N + dy, N), lax.rem(gz + N + dz, N))

    barrier = pltpu.get_barrier_semaphore()

    greeted = [near(dx, dy, dz) for dx in (-1, 1) for dy in (-1, 0, 1) for dz in (-1, 0, 1)]
    greeted += [near(0, dy, dz) for dy in (-1, 1) for dz in (-1, 1)]
    greeted += [near(0, k, 0) for k in range(1, N)] + [near(0, 0, k) for k in range(1, N)]
    for device in greeted:
        pl.semaphore_signal(barrier, inc=1, device_id=device, device_id_type=MESH)

    inner = (pl.ds(W, CX), pl.ds(W, CY))
    local = [
        (e_ref, own.at[0:3]),
        (ep_ref, own.at[3:6]),
        (co_ref, own.at[6]),
        (cell_ref, iport.at[0]),
        (route_ref, iport.at[1]),
        (group_ref, iport.at[2]),
        (gain_ref, fport.at[0]),
        (drive_ref, fport.at[1]),
        (bias_ref, fport.at[2]),
        (couple_ref, fport.at[3]),
        (e_ref, a.at[:, inner[0], inner[1]]),
        (ep_ref, b.at[:, inner[0], inner[1]]),
        (co_ref, c.at[inner[0], inner[1]]),
    ]
    local = [pltpu.make_async_copy(s, d, lsem.at[i]) for i, (s, d) in enumerate(local)]
    for copy in local:
        copy.start()
    for copy in local[:3]:
        copy.wait()

    lane = lax.broadcasted_iota(jnp.int32, (CZ, CZ), 1)
    lane8 = lax.broadcasted_iota(jnp.int32, (8, CZ), 1)
    slot = lane8 % CY // W
    iota8 = lax.broadcasted_iota(jnp.int32, (8, PORTS), 0)

    def turn(v, shift):
        shift = shift % CZ
        return v if shift == 0 else pltpu.roll(v, shift, 1)

    def pack():
        packed = jnp.zeros((CZ, CZ), F32)
        for f in range(7):
            rolled = pltpu.roll(own[f].reshape(CZ, CZ), W + 8 * f, 1)
            packed = jnp.where(lane // 8 == f, rolled, packed)
        packed = packed.T
        rows = [packed[8 * f : 8 * f + 8] for f in range(7)]
        for f in range(7):
            pz[f] = rows[f]

        def quarters(group, top):
            out = turn(group[0], -12 if top else 0)
            for j in range(1, len(group)):
                out = jnp.where(slot == j, turn(group[j], 4 * j - (12 if top else 0)), out)
            return out

        halves = []
        for top in (0, 1):
            tiles = []
            for j in range(4):
                if j == 3:
                    tile = turn(rows[3], 64 * top)
                elif top:
                    tile = jnp.where(lane8 < 64, turn(rows[j], 64), rows[j + 4])
                else:
                    tile = jnp.where(lane8 < 64, rows[j], turn(rows[j + 4], 64))
                px[top, j] = tile
                tiles.append(tile)
            halves.append(tiles)
        for top in (0, 1):
            py[top, 0] = quarters(rows[0:4], top)
            py[top, 1] = quarters(rows[4:7], top)
            for xt in (0, 1):
                pc[xt, top] = quarters(halves[xt], top)

    run("pack", pack)

    for copy in local[3:]:
        copy.wait()
    def ports():
        route = iport[1]
        at64 = lax.broadcasted_iota(jnp.int32, (64, PORTS), 0) == route
        earlier = lax.broadcasted_iota(jnp.int32, (PORTS, PORTS), 0) < lax.broadcasted_iota(
            jnp.int32, (PORTS, PORTS), 1
        )
        count = dot_nn(
            jnp.where(at64, 1.0, 0.0).astype(BF16), jnp.where(earlier, 1.0, 0.0).astype(BF16)
        )
        rank = jnp.sum(jnp.where(at64, count, 0.0), axis=0, keepdims=True).astype(jnp.int32)
        slot_lane = route + 64 * (rank % 2)
        slot_row = rank // 2
        iota128 = lax.broadcasted_iota(jnp.int32, (CZ, PORTS), 0)
        lanem[...] = jnp.where(iota128 == slot_lane, 1.0, 0.0).astype(BF16)
        in_row = iota8 % 4 == slot_row
        rowm[...] = jnp.where(in_row, 1.0, 0.0)
        values = [fport[0], fport[1], fport[2], fport[3], iport[2].astype(F32) + 1.0]
        stacked = jnp.concatenate(
            [
                jnp.where(in_row, jnp.where(iota8 < 4, values[2 * i], values[min(2 * i + 1, 4)]), 0.0)
                for i in range(3)
            ],
            axis=0,
        )
        slots = three(dot_nt, stacked, lanem[...])
        for i in range(NPAR):
            ownpar[i] = slots[4 * i : 4 * i + 4]
        cell = iport[0]
        cellm[...] = jnp.where(iota128 == cell // CZ, 1.0, 0.0).astype(BF16)
        zm[...] = jnp.where(iota128 == cell % CZ, 1.0, 0.0).astype(BF16)

    run("ports", ports)

    pl.semaphore_wait(barrier, len(greeted))
    for k in range(1, N):
        pl.semaphore_signal(plane, inc=1, device_id=near(0, k, 0), device_id_type=MESH)

    def span(d, width, size):
        if d == 0:
            return pl.ds(0, size), pl.ds(W, size)
        if d > 0:
            return pl.ds(size - width, width), pl.ds(W - width, width)
        return pl.ds(0, width), pl.ds(W + size, width)

    halo = []

    def send(src, dst, d):
        i = len(halo)
        copy = pltpu.make_async_remote_copy(
            src_ref=src,
            dst_ref=dst,
            send_sem=hsend.at[i],
            recv_sem=hrecv.at[i],
            device_id=near(*d),
            device_id_type=MESH,
        )
        copy.start()
        halo.append(copy)

    for dz in (1, -1):
        part = pl.ds(0, W) if dz > 0 else pl.ds(W, W)
        send(pz.at[:, part], qz.at[:, part], (0, 0, dz))
        for d in (1, -1):
            mine, theirs = (1, 0) if d > 0 else (0, 1)
            send(px.at[mine, :, part], qx.at[theirs, :, part], (d, 0, dz))
            send(py.at[mine, :, part], qy.at[theirs, :, part], (0, d, dz))
            for dy in (1, -1):
                mine_y, theirs_y = (1, 0) if dy > 0 else (0, 1)
                send(pc.at[mine, mine_y, part], qc.at[theirs, theirs_y, part], (d, dy, dz))
    n_z = len(halo)
    flat = [(0, 1), (0, -1), (1, 0), (-1, 0), (1, 1), (1, -1), (-1, 1), (-1, -1)]
    for dx, dy in flat:
        sx4, tx4 = span(dx, W, CX)
        sy4, ty4 = span(dy, W, CY)
        sx3, tx3 = span(dx, W - 1, CX)
        sy3, ty3 = span(dy, W - 1, CY)
        send(own.at[0:3, sx4, sy4], a.at[:, tx4, ty4], (dx, dy, 0))
        send(own.at[3:6, sx3, sy3], b.at[:, tx3, ty3], (dx, dy, 0))
        send(own.at[6, sx3, sy3], c.at[tx3, ty3], (dx, dy, 0))

    half = pl.ds(4 * lax.rem(gy, 2), 4)
    spread_y = []
    for k in range(1, N):
        copy = pltpu.make_async_remote_copy(
            src_ref=ownpar,
            dst_ref=par.at[gz, gy // 2, :, half],
            send_sem=ysend.at[k - 1],
            recv_sem=yrecv.at[k - 1],
            device_id=(gx, lax.rem(gy + k, N), gz),
            device_id_type=MESH,
        )
        copy.start()
        spread_y.append(copy)
    own_par = pltpu.make_async_copy(ownpar, par.at[gz, gy // 2, :, half], lsem.at[0])
    own_par.start()

    for copy in halo[:n_z]:
        copy.wait_recv()
    low_ok = jnp.where(gz > 0, 1, 0)
    high_ok = jnp.where(gz < N - 1, 1, 0)
    keep = jnp.where(lane < CZ // 2, high_ok, low_ok) == 1

    def unpack(tiles, store):
        block = jnp.concatenate(tiles + [jnp.zeros((CZ - 56, CZ), F32)], axis=0).T
        for f in range(7):
            value = jnp.where(keep, pltpu.roll(block, (CZ - 8 * f - W) % CZ, 1), 0.0)
            ref = (ah, bh, ch)[f // 3]
            store(ref if f == 6 else ref.at[f % 3], value)

    def store_own(ref, value):
        ref[W : W + CX, W : W + CY] = value.reshape(CX, CY, CZ)

    def store_x(ref, value):
        value = value.reshape(CX, CY, CZ)
        ref[0:W, W : W + CY] = value[:W]
        ref[W + CX :, W : W + CY] = value[W:]

    def store_y(ref, value):
        value = value.reshape(CX, 4, W, CZ)
        ref[W : W + CX, 0:W] = value[:, 0]
        ref[W : W + CX, W + CY :] = value[:, 1]
        ref[0:W, 0:W] = value[:W, 2]
        ref[W + CX :, 0:W] = value[W:, 2]
        ref[0:W, W + CY :] = value[:W, 3]
        ref[W + CX :, W + CY :] = value[W:, 3]

    def unpack_all():
        unpack([qz[f] for f in range(7)], store_own)
        tiles = []
        for f in range(7):
            h, j = f // 4, f % 4
            if h == 0:
                tiles.append(jnp.where(lane8 < 64, qx[0, j], pltpu.roll(qx[1, j], 64, 1)))
            else:
                tiles.append(jnp.where(lane8 < 64, pltpu.roll(qx[0, j], 64, 1), qx[1, j]))
        unpack(tiles, store_x)
        tiles = []
        for f in range(7):
            h, j = f // 4, f % 4
            tile = jnp.where(slot == 0, turn(qy[0, h], -4 * j), turn(qy[1, h], 4 - 4 * j))
            for s in (0, 1):
                shift = 8 + 4 * s - 4 * j - 64 * h
                corner = jnp.where(lane8 < 64, turn(qc[0, s], shift), turn(qc[1, s], shift + 64))
                tile = jnp.where(slot == 2 + s, corner, tile)
            tiles.append(tile)
        unpack(tiles, store_y)

    run("unpack", unpack_all)

    def clear(xs, ys):
        for ref in (a, ah, b, bh):
            ref[:, xs, ys] = jnp.zeros_like(ref[:, xs, ys])
        for ref in (c, ch):
            ref[xs, ys] = jnp.zeros_like(ref[xs, ys])

    def clear_y(parts):
        @pl.when(gy == 0)
        def _():
            for xs in parts:
                clear(xs, slice(0, W))

        @pl.when(gy == N - 1)
        def _():
            for xs in parts:
                clear(xs, slice(W + CY, EY))

    for copy in halo[n_z : n_z + 6]:
        copy.wait_recv()
    clear_y([slice(W, W + CX)])

    def early():
        substep(a, ah, b, bh, c, ch, 5, 11, False)
        substep(b, bh, a, ah, c, ch, 6, 10, False)
        substep(a, ah, b, bh, c, ch, 7, 9, False)

    run("early", early)

    own_par.wait()
    for copy in spread_y:
        copy.wait_recv()
    spread_x = []
    for k in range(1, 4):
        copy = pltpu.make_async_remote_copy(
            src_ref=par.at[gz],
            dst_ref=par.at[gz],
            send_sem=xsend.at[k - 1],
            recv_sem=xrecv.at[k - 1],
            device_id=(gx, gy, lax.rem(gz + 2 * k, N)),
            device_id_type=MESH,
        )
        copy.start()
        spread_x.append(copy)

    for copy in halo[n_z + 6 :]:
        copy.wait_recv()
    clear_y([slice(0, W), slice(W + CX, EX)])

    @pl.when(gx == 0)
    def _():
        clear(slice(0, W), slice(0, EY))

    @pl.when(gx == N - 1)
    def _():
        clear(slice(W + CX, EX), slice(0, EY))

    def late():
        substep(a, ah, b, bh, c, ch, 1, 5, False)
        substep(a, ah, b, bh, c, ch, 11, 15, False)
        substep(b, bh, a, ah, c, ch, 2, 6, False)
        substep(b, bh, a, ah, c, ch, 10, 14, False)
        substep(a, ah, b, bh, c, ch, 3, 7, False)
        substep(a, ah, b, bh, c, ch, 9, 13, False)

    run("late", late)
    out_last = pltpu.make_async_copy(b.at[:, inner[0], inner[1]], last_ref, lsem.at[1])
    out_last.start()
    run("step4", lambda: substep(b, bh, a, ah, c, ch, 4, EX - 4, True))
    out_next = pltpu.make_async_copy(
        a.at[0:2, inner[0], inner[1]], next_ref.at[0:2], lsem.at[2]
    )
    out_next.start()

    def take():
        ez = a[2, W : W + CX, W : W + CY].reshape(CZ, CZ)
        picked = three(dot_nn, ez.T, cellm[...])
        sample = jnp.sum(picked * zm[...].astype(F32), axis=0, keepdims=True)
        found = three(dot_nt, rowm[...] * sample, lanem[...])
        sample8[...] = found
        ownsam[...] = found[0:4]

    run("take", take)
    pl.semaphore_wait(plane, N - 1)
    for k in range(1, N * N):
        t = lax.rem(me + k, N * N)
        pltpu.make_async_remote_copy(
            src_ref=ownsam,
            dst_ref=sam.at[gz, gy // 2, half],
            send_sem=ssend,
            recv_sem=srecv,
            device_id=(gx, lax.rem(t, N), t // N),
            device_id_type=MESH,
        ).start()
    own_sam = pltpu.make_async_copy(ownsam, sam.at[gz, gy // 2, half], lsem.at[0])
    own_sam.start()

    for copy in spread_x:
        copy.wait_recv()
    core = lax.rem(gz, 2)
    twins = []
    for i in range(4):
        copy = pltpu.make_async_remote_copy(
            src_ref=par.at[2 * i + core],
            dst_ref=par.at[2 * i + core],
            send_sem=tsem.at[0, i],
            recv_sem=tsem.at[1, i],
            device_id=(gx, gy, gz + 1 - 2 * core),
            device_id_type=MESH,
        )
        copy.start()
        twins.append(copy)
    for copy in twins:
        copy.wait_recv()
    own_sam.wait()
    pltpu.make_async_copy(drain, drain, srecv).wait()

    def solve():
        sub = lax.broadcasted_iota(jnp.int32, (8, CZ), 0)

        def totals(first):
            def add(i, acc):
                for j in range(N // 2):
                    volt = sam[i, j] if first else node[i, j]
                    s = jnp.tanh(volt)
                    grp = par[i, j, 4]
                    acc = tuple(
                        acc[g] + jnp.where(grp == float(g + 1), s, 0.0) for g in range(GROUPS)
                    )
                return acc

            acc = lax.fori_loop(0, N, add, tuple(jnp.zeros((8, CZ), F32) for _ in range(GROUPS)))
            total = jnp.zeros((8, CZ), F32)
            for g in range(GROUPS):
                total = jnp.where(sub == g, jnp.sum(acc[g], axis=0, keepdims=True), total)
            return total + pltpu.roll(total, 64, 1)

        def newton(volt, sample, gain, drive, bias, couple, grp, total):
            s = jnp.tanh(volt)
            shared = jnp.zeros_like(volt)
            for g in range(GROUPS):
                shared = jnp.where(grp == float(g + 1), total[g : g + 1], shared)
            resid = (1.0 + gain) * volt - sample - bias + drive * s + couple * shared
            slope = 1.0 + gain + (drive + couple) * (1.0 - s * s)
            return volt - resid / slope

        mine = sample8[...]
        my = [ownpar[i] for i in range(NPAR)]
        my = [jnp.concatenate([v, v], axis=0) for v in my]
        volt = mine
        for iterate in range(3):
            total = totals(iterate == 0)
            volt = newton(volt, mine, *my, total)
            if iterate < 2:

                def move(i, _):
                    for j in range(N // 2):
                        start = sam[i, j]
                        now = start if iterate == 0 else node[i, j]
                        node[i, j] = newton(
                            now, start, *[par[i, j, p] for p in range(NPAR)], total
                        )
                    return 0

                lax.fori_loop(0, N, move, 0)
        current8[...] = my[0] * (volt - mine)

    run("solve", solve)

    def back():
        spread = three(dot_nn, current8[...], lanem[...])
        port = jnp.sum(jnp.where(iota8 < 4, rowm[...] * spread, 0.0), axis=0, keepdims=True)
        cur_ref[...] = port
        extra = three(dot_nt, cellm[...].astype(F32) * port, zm[...])
        next_ref[2] = (a[2, W : W + CX, W : W + CY].reshape(CZ, CZ) + extra).reshape(CX, CY, CZ)

    run("back", back)
    for copy in (out_last, out_next):
        copy.wait()
    for copy in halo + spread_y + spread_x + twins:
        copy.wait_send()
    pltpu.make_async_copy(drain, drain, ssend).wait()


def on_device(e, ep, co, cell, route, group, gain, drive, bias, couple):
    line = lambda v: v.reshape(1, PORTS)
    any_spec = pl.BlockSpec(memory_space=pl.ANY)
    dma = pltpu.SemaphoreType.DMA
    ext, ext1 = pltpu.VMEM((3, EX, EY, CZ), F32), pltpu.VMEM((EX, EY, CZ), F32)
    electric, last, current = pl.pallas_call(
        kernel,
        out_shape=(
            pltpu.VMEM((3, CX, CY, CZ), F32),
            pltpu.VMEM((3, CX, CY, CZ), F32),
            pltpu.VMEM((1, PORTS), F32),
        ),
        in_specs=[any_spec] * 10,
        out_specs=(pl.BlockSpec(memory_space=pltpu.VMEM),) * 3,
        scratch_shapes=[
            pltpu.VMEM((7, CX, CY, CZ), F32),
            ext,
            ext,
            ext,
            ext,
            ext1,
            ext1,
            pltpu.VMEM((7, 8, CZ), F32),
            pltpu.VMEM((2, 4, 8, CZ), F32),
            pltpu.VMEM((2, 2, 8, CZ), F32),
            pltpu.VMEM((2, 2, 8, CZ), F32),
            pltpu.VMEM((7, 8, CZ), F32),
            pltpu.VMEM((2, 4, 8, CZ), F32),
            pltpu.VMEM((2, 2, 8, CZ), F32),
            pltpu.VMEM((2, 2, 8, CZ), F32),
            pltpu.VMEM((3, 1, PORTS), jnp.int32),
            pltpu.VMEM((4, 1, PORTS), F32),
            pltpu.VMEM((NPAR, 4, CZ), F32),
            pltpu.VMEM((4, CZ), F32),
            pltpu.VMEM((N, N // 2, NPAR, 8, CZ), F32),
            pltpu.VMEM((N, N // 2, 8, CZ), F32),
            pltpu.VMEM((N, N // 2, 8, CZ), F32),
            pltpu.VMEM((N * N - 1, 4, CZ), F32),
            pltpu.VMEM((8, PORTS), F32),
            pltpu.VMEM((CZ, PORTS), BF16),
            pltpu.VMEM((CZ, PORTS), BF16),
            pltpu.VMEM((CZ, PORTS), BF16),
            pltpu.VMEM((8, CZ), F32),
            pltpu.VMEM((8, CZ), F32),
            dma((13,)),
            dma((42,)),
            dma((42,)),
            dma((N - 1,)),
            dma((N - 1,)),
            dma((3,)),
            dma((3,)),
            dma((2, 4)),
            dma,
            dma,
            pltpu.SemaphoreType.REGULAR,
        ],
        compiler_params=pltpu.CompilerParams(
            collective_id=0, has_side_effects=True, vmem_limit_bytes=56 * 1024 * 1024
        ),
    )(e, ep, co, line(cell), line(route), line(group), line(gain), line(drive), line(bias), line(couple))
    return electric, last, current.reshape(PORTS)


def solution(mesh):
    field = P(None, "gx", "gy", "gz")
    port = P(("gx", "gy", "gz"))
    placed = (
        field,
        field,
        P("gx", "gy", "gz"),
        port,
        P(("gx", "gy", "gz"), None),
        port,
        port,
        port,
        port,
        port,
    )
    return jax.shard_map(
        on_device,
        mesh=mesh,
        in_specs=placed,
        out_specs=(field, field, port),
        check_vma=False,
    )
```

```python
import jax
import jax.numpy as jnp
from jax import lax
from jax.experimental import pallas as pl
from jax.experimental.pallas import tpu as pltpu
from jax.sharding import PartitionSpec as P

MESH = pl.DeviceIdType.MESH
F32 = jnp.float32
BF16 = jnp.bfloat16
N = 8
W = 4
CX, CY, CZ = 8, 16, 128
EX, EY = CX + 2 * W, CY + 2 * W
PORTS = 256
GROUPS = 8
NPAR = 5


def pieces(value):
    high = value.astype(BF16).astype(F32)
    rest = value - high
    mid = rest.astype(BF16).astype(F32)
    return high, mid, rest - mid


def dot_nt(a, b):
    return lax.dot_general(a, b, (((1,), (1,)), ((), ())), preferred_element_type=F32)


def dot_nn(a, b):
    return lax.dot_general(a, b, (((1,), (0,)), ((), ())), preferred_element_type=F32)


def three(dot, value, other):
    rows = value.shape[0]
    out = dot(jnp.concatenate(pieces(value), axis=0).astype(BF16), other)
    return (out[:rows] + out[rows : 2 * rows]) + out[2 * rows :]


def run(name, phase):
    phase()


def up_z(main, halo, lane):
    rm, rh = pltpu.roll(main, CZ - 1, 1), pltpu.roll(halo, CZ - 1, 1)
    return jnp.where(lane == CZ - 1, rh, rm), jnp.where(lane == CZ - 1, rm, rh)


def down_z(main, halo, lane):
    rm, rh = pltpu.roll(main, 1, 1), pltpu.roll(halo, 1, 1)
    return jnp.where(lane == 0, rh, rm), jnp.where(lane == 0, rm, rh)


def up_y(v):
    return pltpu.roll(v, EY - 1, 0)


def down_y(v):
    return pltpu.roll(v, 1, 0)


def substep(now, now_h, old, old_h, cou, cou_h, low, high, last):
    lane = lax.broadcasted_iota(jnp.int32, (EY, CZ), 1)

    def curls(x):
        vx, vy, vz = now[0, x, 0:EY], now[1, x, 0:EY], now[2, x, 0:EY]
        vxh, vyh, vzh = now_h[0, x, 0:EY], now_h[1, x, 0:EY], now_h[2, x, 0:EY]
        vxu, vxuh = up_z(vx, vxh, lane)
        gy = (vxu - vx) - (now[2, x + 1, 0:EY] - vz)
        gyh = (vxuh - vxh) - (now_h[2, x + 1, 0:EY] - vzh)
        gz = (now[1, x + 1, 0:EY] - vy) - (now[0, x, 1 : EY + 1] - vx)
        gzh = (now_h[1, x + 1, 0:EY] - vyh) - (now_h[0, x, 1 : EY + 1] - vxh)
        return gy, gyh, gz, gzh

    def body(x, carry):
        gyp, gyph, gzp, gzph = carry
        vx, vy, vz = now[0, x, 0:EY], now[1, x, 0:EY], now[2, x, 0:EY]
        vxh, vyh, vzh = now_h[0, x, 0:EY], now_h[1, x, 0:EY], now_h[2, x, 0:EY]
        gy, gyh, gz, gzh = curls(x)
        vyu, vyuh = up_z(vy, vyh, lane)
        gx = (now[2, x, 1 : EY + 1] - vz) - (vyu - vy)
        gxh = (now_h[2, x, 1 : EY + 1] - vzh) - (vyuh - vyh)
        gxd, gxdh = down_z(gx, gxh, lane)
        gyd, gydh = down_z(gy, gyh, lane)
        c = cou[x, 0:EY]
        kx = (gz - down_y(gz)) - (gy - gyd)
        ky = (gx - gxd) - (gz - gzp)
        kz = (gy - gyp) - (gx - down_y(gx))
        old[0, x, 0:EY] = 2.0 * vx - old[0, x, 0:EY] - c * kx
        old[1, x, 0:EY] = 2.0 * vy - old[1, x, 0:EY] - c * ky
        old[2, x, 0:EY] = 2.0 * vz - old[2, x, 0:EY] - c * kz
        if not last:
            ch = cou_h[x, 0:EY]
            kxh = (gzh - down_y(gzh)) - (gyh - gydh)
            kyh = (gxh - gxdh) - (gzh - gzph)
            kzh = (gyh - gyph) - (gxh - down_y(gxh))
            old_h[0, x, 0:EY] = 2.0 * vxh - old_h[0, x, 0:EY] - ch * kxh
            old_h[1, x, 0:EY] = 2.0 * vyh - old_h[1, x, 0:EY] - ch * kyh
            old_h[2, x, 0:EY] = 2.0 * vzh - old_h[2, x, 0:EY] - ch * kzh
        return gy, gyh, gz, gzh

    carry = curls(low - 1)
    for x in range(low, high):
        carry = body(x, carry)


def kernel(
    e_ref,
    ep_ref,
    co_ref,
    cell_ref,
    route_ref,
    group_ref,
    gain_ref,
    drive_ref,
    bias_ref,
    couple_ref,
    next_ref,
    last_ref,
    cur_ref,
    own,
    a,
    ah,
    b,
    bh,
    c,
    ch,
    pz,
    px,
    py,
    pc,
    qz,
    qx,
    qy,
    qc,
    iport,
    fport,
    ownpar,
    ownsam,
    par,
    sam,
    node,
    drain,
    rowm,
    lanem,
    cellm,
    zm,
    sample8,
    current8,
    lsem,
    hsend,
    hrecv,
    ysend,
    yrecv,
    xsend,
    xrecv,
    tsem,
    ssend,
    srecv,
    plane,
):
    gx, gy, gz = lax.axis_index("gx"), lax.axis_index("gy"), lax.axis_index("gz")

    def near(dx, dy, dz):
        return (lax.rem(gx + N + dx, N), lax.rem(gy + N + dy, N), lax.rem(gz + N + dz, N))

    inner = (pl.ds(W, CX), pl.ds(W, CY))
    local = [
        (e_ref, own.at[0:3]),
        (ep_ref, own.at[3:6]),
        (co_ref, own.at[6]),
        (cell_ref, iport.at[0]),
        (route_ref, iport.at[1]),
        (group_ref, iport.at[2]),
        (gain_ref, fport.at[0]),
        (drive_ref, fport.at[1]),
        (bias_ref, fport.at[2]),
        (couple_ref, fport.at[3]),
        (e_ref, a.at[:, inner[0], inner[1]]),
        (ep_ref, b.at[:, inner[0], inner[1]]),
        (co_ref, c.at[inner[0], inner[1]]),
    ]
    local = [pltpu.make_async_copy(s, d, lsem.at[i]) for i, (s, d) in enumerate(local)]
    for copy in local[:3]:
        copy.start()

    barrier = pltpu.get_barrier_semaphore()

    greeted = [near(0, dy, dz) for dy in (-1, 1) for dz in (-1, 1)]
    greeted += [near(0, k, 0) for k in range(1, N)] + [near(0, 0, k) for k in range(1, N)]

    def has(d):
        return gx < N - 1 if d > 0 else gx > 0

    def greet(device):
        pl.semaphore_signal(barrier, inc=1, device_id=device, device_id_type=MESH)

    for dx in (-1, 1):

        @pl.when(has(dx))
        def _():
            for dy in (-1, 0, 1):
                for dz in (-1, 0, 1):
                    greet(near(dx, dy, dz))

    for device in greeted:
        greet(device)

    for copy in local[3:]:
        copy.start()
    for copy in local[:3]:
        copy.wait()

    lane = lax.broadcasted_iota(jnp.int32, (CZ, CZ), 1)
    lane8 = lax.broadcasted_iota(jnp.int32, (8, CZ), 1)
    slot = lane8 % CY // W
    iota8 = lax.broadcasted_iota(jnp.int32, (8, PORTS), 0)

    def turn(v, shift):
        shift = shift % CZ
        return v if shift == 0 else pltpu.roll(v, shift, 1)

    def pack():
        packed = jnp.zeros((CZ, CZ), F32)
        for f in range(7):
            rolled = pltpu.roll(own[f].reshape(CZ, CZ), W + 8 * f, 1)
            packed = jnp.where(lane // 8 == f, rolled, packed)
        packed = packed.T
        rows = [packed[8 * f : 8 * f + 8] for f in range(7)]
        for f in range(7):
            pz[f] = rows[f]

        def quarters(group, top):
            out = turn(group[0], -12 if top else 0)
            for j in range(1, len(group)):
                out = jnp.where(slot == j, turn(group[j], 4 * j - (12 if top else 0)), out)
            return out

        halves = []
        for top in (0, 1):
            tiles = []
            for j in range(4):
                if j == 3:
                    tile = turn(rows[3], 64 * top)
                elif top:
                    tile = jnp.where(lane8 < 64, turn(rows[j], 64), rows[j + 4])
                else:
                    tile = jnp.where(lane8 < 64, rows[j], turn(rows[j + 4], 64))
                px[top, j] = tile
                tiles.append(tile)
            halves.append(tiles)
        for top in (0, 1):
            py[top, 0] = quarters(rows[0:4], top)
            py[top, 1] = quarters(rows[4:7], top)
            for xt in (0, 1):
                pc[xt, top] = quarters(halves[xt], top)

    run("pack", pack)

    beside = jnp.where(gx > 0, 9, 0) + jnp.where(gx < N - 1, 9, 0)
    pl.semaphore_wait(barrier, len(greeted) + beside)
    for k in range(1, N):
        pl.semaphore_signal(plane, inc=1, device_id=near(0, k, 0), device_id_type=MESH)

    def span(d, width, size):
        if d == 0:
            return pl.ds(0, size), pl.ds(W, size)
        if d > 0:
            return pl.ds(size - width, width), pl.ds(W - width, width)
        return pl.ds(0, width), pl.ds(W + size, width)

    halo = []

    def send(src, dst, d):
        i = len(halo)
        copy = pltpu.make_async_remote_copy(
            src_ref=src,
            dst_ref=dst,
            send_sem=hsend.at[i],
            recv_sem=hrecv.at[i],
            device_id=near(*d),
            device_id_type=MESH,
        )
        if d[0]:
            pl.when(has(d[0]))(copy.start)
        else:
            copy.start()
        halo.append((copy, d[0]))

    def received(copies):
        for copy, d in copies:
            if d:
                pl.when(has(-d))(copy.wait_recv)
            else:
                copy.wait_recv()

    for dz in (1, -1):
        part = pl.ds(0, W) if dz > 0 else pl.ds(W, W)
        send(pz.at[:, part], qz.at[:, part], (0, 0, dz))
        for d in (1, -1):
            mine, theirs = (1, 0) if d > 0 else (0, 1)
            send(px.at[mine, :, part], qx.at[theirs, :, part], (d, 0, dz))
            send(py.at[mine, :, part], qy.at[theirs, :, part], (0, d, dz))
            for dy in (1, -1):
                mine_y, theirs_y = (1, 0) if dy > 0 else (0, 1)
                send(pc.at[mine, mine_y, part], qc.at[theirs, theirs_y, part], (d, dy, dz))
    n_z = len(halo)
    flat = [(0, 1), (0, -1), (1, 0), (-1, 0), (1, 1), (1, -1), (-1, 1), (-1, -1)]
    for dx, dy in flat:
        sx4, tx4 = span(dx, W, CX)
        sy4, ty4 = span(dy, W, CY)
        sx3, tx3 = span(dx, W - 1, CX)
        sy3, ty3 = span(dy, W - 1, CY)
        if dx and dy:
            for near_x, near_y in ((2, W), (W, 2)):
                skip = 2 if near_x == W else 0
                xs = pl.ds(CX - near_x, near_x - skip) if dx > 0 else pl.ds(skip, near_x - skip)
                xt = pl.ds(W - near_x, near_x - skip) if dx > 0 else pl.ds(W + CX + skip, near_x - skip)
                ys, yt = span(dy, near_y, CY)
                send(own.at[0:3, xs, ys], a.at[:, xt, yt], (dx, dy, 0))
            send(own.at[3:6, sx3, sy3], b.at[:, tx3, ty3], (dx, dy, 0))
            send(own.at[6, sx3, sy3], c.at[tx3, ty3], (dx, dy, 0))
            continue
        send(own.at[0:3, sx4, sy4], a.at[:, tx4, ty4], (dx, dy, 0))
        send(own.at[3:6, sx3, sy3], b.at[:, tx3, ty3], (dx, dy, 0))
        send(own.at[6, sx3, sy3], c.at[tx3, ty3], (dx, dy, 0))

    for copy in local[3:]:
        copy.wait()
    def ports():
        route = iport[1]
        at64 = lax.broadcasted_iota(jnp.int32, (64, PORTS), 0) == route
        earlier = lax.broadcasted_iota(jnp.int32, (PORTS, PORTS), 0) < lax.broadcasted_iota(
            jnp.int32, (PORTS, PORTS), 1
        )
        count = dot_nn(
            jnp.where(at64, 1.0, 0.0).astype(BF16), jnp.where(earlier, 1.0, 0.0).astype(BF16)
        )
        rank = jnp.sum(jnp.where(at64, count, 0.0), axis=0, keepdims=True).astype(jnp.int32)
        slot_lane = route + 64 * (rank % 2)
        slot_row = rank // 2
        iota128 = lax.broadcasted_iota(jnp.int32, (CZ, PORTS), 0)
        lanem[...] = jnp.where(iota128 == slot_lane, 1.0, 0.0).astype(BF16)
        in_row = iota8 % 4 == slot_row
        rowm[...] = jnp.where(in_row, 1.0, 0.0)
        values = [fport[0], fport[1], fport[2], fport[3], iport[2].astype(F32) + 1.0]
        stacked = jnp.concatenate(
            [
                jnp.where(in_row, jnp.where(iota8 < 4, values[2 * i], values[min(2 * i + 1, 4)]), 0.0)
                for i in range(3)
            ],
            axis=0,
        )
        slots = three(dot_nt, stacked, lanem[...])
        for i in range(NPAR):
            ownpar[i] = slots[4 * i : 4 * i + 4]
        cell = iport[0]
        cellm[...] = jnp.where(iota128 == cell // CZ, 1.0, 0.0).astype(BF16)
        zm[...] = jnp.where(iota128 == cell % CZ, 1.0, 0.0).astype(BF16)

    run("ports", ports)

    half = pl.ds(4 * lax.rem(gy, 2), 4)
    spread_y = []
    for k in range(1, N):
        copy = pltpu.make_async_remote_copy(
            src_ref=ownpar,
            dst_ref=par.at[gz, gy // 2, :, half],
            send_sem=ysend.at[k - 1],
            recv_sem=yrecv.at[k - 1],
            device_id=(gx, lax.rem(gy + k, N), gz),
            device_id_type=MESH,
        )
        copy.start()
        spread_y.append(copy)
    own_par = pltpu.make_async_copy(ownpar, par.at[gz, gy // 2, :, half], lsem.at[0])
    own_par.start()

    received(halo[:n_z])
    low_ok = jnp.where(gz > 0, 1, 0)
    high_ok = jnp.where(gz < N - 1, 1, 0)
    keep = jnp.where(lane < CZ // 2, high_ok, low_ok) == 1

    def unpack(tiles, store):
        block = jnp.concatenate(tiles + [jnp.zeros((CZ - 56, CZ), F32)], axis=0).T
        for f in range(7):
            value = jnp.where(keep, pltpu.roll(block, (CZ - 8 * f - W) % CZ, 1), 0.0)
            ref = (ah, bh, ch)[f // 3]
            store(ref if f == 6 else ref.at[f % 3], value)

    def store_own(ref, value):
        ref[W : W + CX, W : W + CY] = value.reshape(CX, CY, CZ)

    def store_x(ref, value):
        value = value.reshape(CX, CY, CZ)
        ref[0:W, W : W + CY] = value[:W]
        ref[W + CX :, W : W + CY] = value[W:]

    def store_y(ref, value):
        value = value.reshape(CX, 4, W, CZ)
        ref[W : W + CX, 0:W] = value[:, 0]
        ref[W : W + CX, W + CY : EY] = value[:, 1]
        ref[0:W, 0:W] = value[:W, 2]
        ref[W + CX :, 0:W] = value[W:, 2]
        ref[0:W, W + CY : EY] = value[:W, 3]
        ref[W + CX :, W + CY : EY] = value[W:, 3]

    def unpack_all():
        unpack([qz[f] for f in range(7)], store_own)
        tiles = []
        for f in range(7):
            h, j = f // 4, f % 4
            if h == 0:
                tiles.append(jnp.where(lane8 < 64, qx[0, j], pltpu.roll(qx[1, j], 64, 1)))
            else:
                tiles.append(jnp.where(lane8 < 64, pltpu.roll(qx[0, j], 64, 1), qx[1, j]))
        unpack(tiles, store_x)
        tiles = []
        for f in range(7):
            h, j = f // 4, f % 4
            tile = jnp.where(slot == 0, turn(qy[0, h], -4 * j), turn(qy[1, h], 4 - 4 * j))
            for s in (0, 1):
                shift = 8 + 4 * s - 4 * j - 64 * h
                corner = jnp.where(lane8 < 64, turn(qc[0, s], shift), turn(qc[1, s], shift + 64))
                tile = jnp.where(slot == 2 + s, corner, tile)
            tiles.append(tile)
        unpack(tiles, store_y)

    run("unpack", unpack_all)

    def clear(xs, ys):
        for ref in (a, ah, b, bh):
            ref[:, xs, ys] = jnp.zeros_like(ref[:, xs, ys])
        for ref in (c, ch):
            ref[xs, ys] = jnp.zeros_like(ref[xs, ys])

    def clear_y(parts):
        @pl.when(gy == 0)
        def _():
            for xs in parts:
                clear(xs, slice(0, W))

        @pl.when(gy == N - 1)
        def _():
            for xs in parts:
                clear(xs, slice(W + CY, EY))

    received(halo[n_z : n_z + 6])
    clear_y([slice(W, W + CX)])

    def early():
        substep(a, ah, b, bh, c, ch, 5, 11, False)
        substep(b, bh, a, ah, c, ch, 6, 10, False)
        substep(a, ah, b, bh, c, ch, 7, 9, False)

    run("early", early)

    own_par.wait()
    for copy in spread_y:
        copy.wait_recv()
    spread_x = []
    for k in range(1, 4):
        copy = pltpu.make_async_remote_copy(
            src_ref=par.at[gz],
            dst_ref=par.at[gz],
            send_sem=xsend.at[k - 1],
            recv_sem=xrecv.at[k - 1],
            device_id=(gx, gy, lax.rem(gz + 2 * k, N)),
            device_id_type=MESH,
        )
        copy.start()
        spread_x.append(copy)

    received(halo[n_z + 6 :])
    clear_y([slice(0, W), slice(W + CX, EX)])

    @pl.when(gx == 0)
    def _():
        clear(slice(0, W), slice(0, EY))

    @pl.when(gx == N - 1)
    def _():
        clear(slice(W + CX, EX), slice(0, EY))

    def late():
        substep(a, ah, b, bh, c, ch, 1, 5, False)
        substep(a, ah, b, bh, c, ch, 11, 15, False)
        substep(b, bh, a, ah, c, ch, 2, 6, False)
        substep(b, bh, a, ah, c, ch, 10, 14, False)
        substep(a, ah, b, bh, c, ch, 3, 7, False)
        substep(a, ah, b, bh, c, ch, 9, 13, False)

    run("late", late)
    out_last = pltpu.make_async_copy(b.at[:, inner[0], inner[1]], last_ref, lsem.at[1])
    out_last.start()
    run("step4", lambda: substep(b, bh, a, ah, c, ch, 4, EX - 4, True))
    out_next = pltpu.make_async_copy(
        a.at[0:2, inner[0], inner[1]], next_ref.at[0:2], lsem.at[2]
    )
    out_next.start()

    def take():
        ez = a[2, W : W + CX, W : W + CY].reshape(CZ, CZ)
        picked = three(dot_nn, ez.T, cellm[...])
        sample = jnp.sum(picked * zm[...].astype(F32), axis=0, keepdims=True)
        found = three(dot_nt, rowm[...] * sample, lanem[...])
        sample8[...] = found
        ownsam[...] = found[0:4]

    run("take", take)
    pl.semaphore_wait(plane, N - 1)
    hops = lambda ky, kz: min(ky, N - ky) + min(kz, N - kz) / 2
    others = [(ky, kz) for ky in range(N) for kz in range(N) if ky or kz]
    for ky, kz in sorted(others, key=lambda k: -hops(*k)):
        pltpu.make_async_remote_copy(
            src_ref=ownsam,
            dst_ref=sam.at[gz, gy // 2, half],
            send_sem=ssend,
            recv_sem=srecv,
            device_id=near(0, ky, kz),
            device_id_type=MESH,
        ).start()
    own_sam = pltpu.make_async_copy(ownsam, sam.at[gz, gy // 2, half], lsem.at[0])
    own_sam.start()

    for copy in spread_x:
        copy.wait_recv()
    core = lax.rem(gz, 2)
    twins = []
    for i in range(4):
        copy = pltpu.make_async_remote_copy(
            src_ref=par.at[2 * i + core],
            dst_ref=par.at[2 * i + core],
            send_sem=tsem.at[0, i],
            recv_sem=tsem.at[1, i],
            device_id=(gx, gy, gz + 1 - 2 * core),
            device_id_type=MESH,
        )
        copy.start()
        twins.append(copy)
    for copy in twins:
        copy.wait_recv()
    own_sam.wait()
    pltpu.make_async_copy(drain, drain, srecv).wait()

    def solve():
        sub = lax.broadcasted_iota(jnp.int32, (8, CZ), 0)

        def totals(first):
            def add(i, acc):
                for j in range(N // 2):
                    volt = sam[i, j] if first else node[i, j]
                    s = jnp.tanh(volt)
                    grp = par[i, j, 4]
                    acc = tuple(
                        acc[g] + jnp.where(grp == float(g + 1), s, 0.0) for g in range(GROUPS)
                    )
                return acc

            acc = lax.fori_loop(0, N, add, tuple(jnp.zeros((8, CZ), F32) for _ in range(GROUPS)))
            total = jnp.zeros((8, CZ), F32)
            for g in range(GROUPS):
                total = jnp.where(sub == g, jnp.sum(acc[g], axis=0, keepdims=True), total)
            return total + pltpu.roll(total, 64, 1)

        def newton(volt, sample, gain, drive, bias, couple, grp, total):
            s = jnp.tanh(volt)
            which = jnp.maximum(grp.astype(jnp.int32) - 1, 0)
            shared = jnp.take_along_axis(total, which, axis=0, mode="promise_in_bounds")
            resid = (1.0 + gain) * volt - sample - bias + drive * s + couple * shared
            slope = 1.0 + gain + (drive + couple) * (1.0 - s * s)
            return volt - resid / slope

        mine = sample8[...]
        my = [ownpar[i] for i in range(NPAR)]
        my = [jnp.concatenate([v, v], axis=0) for v in my]
        volt = mine
        for iterate in range(3):
            total = totals(iterate == 0)
            volt = newton(volt, mine, *my, total)
            if iterate < 2:

                def move(i, _):
                    for j in range(N // 2):
                        start = sam[i, j]
                        now = start if iterate == 0 else node[i, j]
                        node[i, j] = newton(
                            now, start, *[par[i, j, p] for p in range(NPAR)], total
                        )
                    return 0

                lax.fori_loop(0, N, move, 0)
        current8[...] = my[0] * (volt - mine)

    run("solve", solve)

    def back():
        spread = three(dot_nn, current8[...], lanem[...])
        port = jnp.sum(jnp.where(iota8 < 4, rowm[...] * spread, 0.0), axis=0, keepdims=True)
        cur_ref[...] = port
        extra = three(dot_nt, cellm[...].astype(F32) * port, zm[...])
        next_ref[2] = (a[2, W : W + CX, W : W + CY].reshape(CZ, CZ) + extra).reshape(CX, CY, CZ)

    run("back", back)
    for copy in (out_last, out_next):
        copy.wait()
    for copy, d in halo:
        if d:
            pl.when(has(d))(copy.wait_send)
        else:
            copy.wait_send()
    for copy in spread_y + spread_x + twins:
        copy.wait_send()
    pltpu.make_async_copy(drain, drain, ssend).wait()


def put_out(e_ref, last_ref, cur_ref, e_out, last_out, cur_out, sem):
    pairs = ((e_ref, e_out), (last_ref, last_out), (cur_ref, cur_out))
    copies = [pltpu.make_async_copy(s, d, sem.at[i]) for i, (s, d) in enumerate(pairs)]
    for copy in copies:
        copy.start()
    for copy in copies:
        copy.wait()


def on_device(e, ep, co, cell, route, group, gain, drive, bias, couple):
    line = lambda v: v.reshape(1, PORTS)
    any_spec = pl.BlockSpec(memory_space=pl.ANY)
    dma = pltpu.SemaphoreType.DMA
    ext, ext1 = pltpu.VMEM((3, EX, EY + 8, CZ), F32), pltpu.VMEM((EX, EY + 8, CZ), F32)
    electric, last, current = pl.pallas_call(
        kernel,
        out_shape=(
            pltpu.VMEM((3, CX, CY, CZ), F32),
            pltpu.VMEM((3, CX, CY, CZ), F32),
            pltpu.VMEM((1, PORTS), F32),
        ),
        in_specs=[any_spec] * 10,
        out_specs=(pl.BlockSpec(memory_space=pltpu.VMEM),) * 3,
        scratch_shapes=[
            pltpu.VMEM((7, CX, CY, CZ), F32),
            ext,
            ext,
            ext,
            ext,
            ext1,
            ext1,
            pltpu.VMEM((7, 8, CZ), F32),
            pltpu.VMEM((2, 4, 8, CZ), F32),
            pltpu.VMEM((2, 2, 8, CZ), F32),
            pltpu.VMEM((2, 2, 8, CZ), F32),
            pltpu.VMEM((7, 8, CZ), F32),
            pltpu.VMEM((2, 4, 8, CZ), F32),
            pltpu.VMEM((2, 2, 8, CZ), F32),
            pltpu.VMEM((2, 2, 8, CZ), F32),
            pltpu.VMEM((3, 1, PORTS), jnp.int32),
            pltpu.VMEM((4, 1, PORTS), F32),
            pltpu.VMEM((NPAR, 4, CZ), F32),
            pltpu.VMEM((4, CZ), F32),
            pltpu.VMEM((N, N // 2, NPAR, 8, CZ), F32),
            pltpu.VMEM((N, N // 2, 8, CZ), F32),
            pltpu.VMEM((N, N // 2, 8, CZ), F32),
            pltpu.VMEM((N * N - 1, 4, CZ), F32),
            pltpu.VMEM((8, PORTS), F32),
            pltpu.VMEM((CZ, PORTS), BF16),
            pltpu.VMEM((CZ, PORTS), BF16),
            pltpu.VMEM((CZ, PORTS), BF16),
            pltpu.VMEM((8, CZ), F32),
            pltpu.VMEM((8, CZ), F32),
            dma((13,)),
            dma((46,)),
            dma((46,)),
            dma((N - 1,)),
            dma((N - 1,)),
            dma((3,)),
            dma((3,)),
            dma((2, 4)),
            dma,
            dma,
            pltpu.SemaphoreType.REGULAR,
        ],
        compiler_params=pltpu.CompilerParams(
            collective_id=0, has_side_effects=True, vmem_limit_bytes=56 * 1024 * 1024
        ),
    )(e, ep, co, line(cell), line(route), line(group), line(gain), line(drive), line(bias), line(couple))
    return pl.pallas_call(
        put_out,
        out_shape=(
            jax.ShapeDtypeStruct((3, CX, CY, CZ), F32),
            jax.ShapeDtypeStruct((3, CX, CY, CZ), F32),
            jax.ShapeDtypeStruct((PORTS,), F32),
        ),
        in_specs=[any_spec] * 3,
        out_specs=(any_spec,) * 3,
        scratch_shapes=[dma((3,))],
        compiler_params=pltpu.CompilerParams(vmem_limit_bytes=1024 * 1024),
    )(electric, last, current.reshape(PORTS))


def solution(mesh):
    field = P(None, "gx", "gy", "gz")
    port = P(("gx", "gy", "gz"))
    placed = (
        field,
        field,
        P("gx", "gy", "gz"),
        port,
        P(("gx", "gy", "gz"), None),
        port,
        port,
        port,
        port,
        port,
    )
    return jax.shard_map(
        on_device,
        mesh=mesh,
        in_specs=placed,
        out_specs=(field, field, port),
        check_vma=False,
    )
```

```python
import jax
import jax.numpy as jnp
from jax import lax
from jax.experimental import pallas as pl
from jax.experimental.pallas import tpu as pltpu
from jax.sharding import PartitionSpec as P

MESH = pl.DeviceIdType.MESH
F32 = jnp.float32
BF16 = jnp.bfloat16
N = 8
W = 4
CX, CY, CZ = 8, 16, 128
EX, EY = CX + 2 * W, CY + 2 * W
PORTS = 256
GROUPS = 8
NPAR = 5


def pieces(value):
    high = value.astype(BF16).astype(F32)
    rest = value - high
    mid = rest.astype(BF16).astype(F32)
    return high, mid, rest - mid


def dot_nt(a, b):
    return lax.dot_general(a, b, (((1,), (1,)), ((), ())), preferred_element_type=F32)


def dot_nn(a, b):
    return lax.dot_general(a, b, (((1,), (0,)), ((), ())), preferred_element_type=F32)


def three(dot, value, other):
    rows = value.shape[0]
    out = dot(jnp.concatenate(pieces(value), axis=0).astype(BF16), other)
    return (out[:rows] + out[rows : 2 * rows]) + out[2 * rows :]


def run(name, phase):
    phase()


def up_z(main, halo, lane):
    rm, rh = pltpu.roll(main, CZ - 1, 1), pltpu.roll(halo, CZ - 1, 1)
    return jnp.where(lane == CZ - 1, rh, rm), jnp.where(lane == CZ - 1, rm, rh)


def down_z(main, halo, lane):
    rm, rh = pltpu.roll(main, 1, 1), pltpu.roll(halo, 1, 1)
    return jnp.where(lane == 0, rh, rm), jnp.where(lane == 0, rm, rh)


def up_y(v):
    return pltpu.roll(v, EY - 1, 0)


def down_y(v):
    return pltpu.roll(v, 1, 0)


def substep(now, now_h, old, old_h, cou, cou_h, low, high, last):
    lane = lax.broadcasted_iota(jnp.int32, (EY, CZ), 1)

    def curls(x):
        vx, vy, vz = now[0, x, 0:EY], now[1, x, 0:EY], now[2, x, 0:EY]
        vxh, vyh, vzh = now_h[0, x, 0:EY], now_h[1, x, 0:EY], now_h[2, x, 0:EY]
        vxu, vxuh = up_z(vx, vxh, lane)
        gy = (vxu - vx) - (now[2, x + 1, 0:EY] - vz)
        gyh = (vxuh - vxh) - (now_h[2, x + 1, 0:EY] - vzh)
        gz = (now[1, x + 1, 0:EY] - vy) - (now[0, x, 1 : EY + 1] - vx)
        gzh = (now_h[1, x + 1, 0:EY] - vyh) - (now_h[0, x, 1 : EY + 1] - vxh)
        return gy, gyh, gz, gzh

    def body(x, carry):
        gyp, gyph, gzp, gzph = carry
        vx, vy, vz = now[0, x, 0:EY], now[1, x, 0:EY], now[2, x, 0:EY]
        vxh, vyh, vzh = now_h[0, x, 0:EY], now_h[1, x, 0:EY], now_h[2, x, 0:EY]
        gy, gyh, gz, gzh = curls(x)
        vyu, vyuh = up_z(vy, vyh, lane)
        gx = (now[2, x, 1 : EY + 1] - vz) - (vyu - vy)
        gxh = (now_h[2, x, 1 : EY + 1] - vzh) - (vyuh - vyh)
        gxd, gxdh = down_z(gx, gxh, lane)
        gyd, gydh = down_z(gy, gyh, lane)
        c = cou[x, 0:EY]
        kx = (gz - down_y(gz)) - (gy - gyd)
        ky = (gx - gxd) - (gz - gzp)
        kz = (gy - gyp) - (gx - down_y(gx))
        old[0, x, 0:EY] = 2.0 * vx - old[0, x, 0:EY] - c * kx
        old[1, x, 0:EY] = 2.0 * vy - old[1, x, 0:EY] - c * ky
        if not last:
            old[2, x, 0:EY] = 2.0 * vz - old[2, x, 0:EY] - c * kz
            ch = cou_h[x, 0:EY]
            kxh = (gzh - down_y(gzh)) - (gyh - gydh)
            kyh = (gxh - gxdh) - (gzh - gzph)
            kzh = (gyh - gyph) - (gxh - down_y(gxh))
            old_h[0, x, 0:EY] = 2.0 * vxh - old_h[0, x, 0:EY] - ch * kxh
            old_h[1, x, 0:EY] = 2.0 * vyh - old_h[1, x, 0:EY] - ch * kyh
            old_h[2, x, 0:EY] = 2.0 * vzh - old_h[2, x, 0:EY] - ch * kzh
        return gy, gyh, gz, gzh

    carry = curls(low - 1)
    for x in range(low, high):
        carry = body(x, carry)


def last_z(now, now_h, old, cou):
    lane = lax.broadcasted_iota(jnp.int32, (CY, CZ), 1)
    mid, below = slice(W, W + CY), slice(W - 1, W + CY - 1)

    def forward(k, x, rows):
        main, halo = now[k, x, rows], now_h[k, x, rows]
        ahead = jnp.where(lane == CZ - 1, pltpu.roll(halo, CZ - 1, 1), pltpu.roll(main, CZ - 1, 1))
        return ahead - main

    def curl_y(x):
        return forward(0, x, mid) - (now[2, x + 1, mid] - now[2, x, mid])

    gyp = curl_y(W - 1)
    for x in range(W, W + CX):
        vz = now[2, x, mid]
        gx = (now[2, x, W + 1 : W + CY + 1] - vz) - forward(1, x, mid)
        gxd = (vz - now[2, x, below]) - forward(1, x, below)
        gy = curl_y(x)
        old[2, x, mid] = 2.0 * vz - old[2, x, mid] - cou[x, mid] * ((gy - gyp) - (gx - gxd))
        gyp = gy


def kernel(
    e_ref,
    ep_ref,
    co_ref,
    cell_ref,
    route_ref,
    group_ref,
    gain_ref,
    drive_ref,
    bias_ref,
    couple_ref,
    next_ref,
    last_ref,
    cur_ref,
    own,
    a,
    ah,
    b,
    bh,
    c,
    ch,
    pz,
    px,
    py,
    pc,
    qz,
    qx,
    qy,
    qc,
    iport,
    fport,
    ownpar,
    ownsam,
    par,
    sam,
    node,
    drain,
    rowm,
    lanem,
    cellm,
    zm,
    sample8,
    current8,
    lsem,
    hsend,
    hrecv,
    ysend,
    yrecv,
    xsend,
    xrecv,
    tsem,
    ssend,
    srecv,
    plane,
):
    gx, gy, gz = lax.axis_index("gx"), lax.axis_index("gy"), lax.axis_index("gz")

    def near(dx, dy, dz):
        return (lax.rem(gx + N + dx, N), lax.rem(gy + N + dy, N), lax.rem(gz + N + dz, N))

    inner = (pl.ds(W, CX), pl.ds(W, CY))
    local = [
        (e_ref, own.at[0:3]),
        (ep_ref, own.at[3:6]),
        (co_ref, own.at[6]),
        (cell_ref, iport.at[0]),
        (route_ref, iport.at[1]),
        (group_ref, iport.at[2]),
        (gain_ref, fport.at[0]),
        (drive_ref, fport.at[1]),
        (bias_ref, fport.at[2]),
        (couple_ref, fport.at[3]),
        (e_ref, a.at[:, inner[0], inner[1]]),
        (ep_ref, b.at[:, inner[0], inner[1]]),
        (co_ref, c.at[inner[0], inner[1]]),
    ]
    local = [pltpu.make_async_copy(s, d, lsem.at[i]) for i, (s, d) in enumerate(local)]
    for copy in local[:3]:
        copy.start()

    barrier = pltpu.get_barrier_semaphore()

    greeted = [near(0, dy, dz) for dy in (-1, 1) for dz in (-1, 1)]
    greeted += [near(0, k, 0) for k in range(1, N)] + [near(0, 0, k) for k in range(1, N)]

    def has(d):
        return gx < N - 1 if d > 0 else gx > 0

    def greet(device):
        pl.semaphore_signal(barrier, inc=1, device_id=device, device_id_type=MESH)

    for dx in (-1, 1):

        @pl.when(has(dx))
        def _():
            for dy in (-1, 0, 1):
                for dz in (-1, 0, 1):
                    greet(near(dx, dy, dz))

    for device in greeted:
        greet(device)

    for copy in local[3:]:
        copy.start()
    for copy in local[:3]:
        copy.wait()

    lane = lax.broadcasted_iota(jnp.int32, (CZ, CZ), 1)
    lane8 = lax.broadcasted_iota(jnp.int32, (8, CZ), 1)
    slot = lane8 % CY // W
    iota8 = lax.broadcasted_iota(jnp.int32, (8, PORTS), 0)

    def turn(v, shift):
        shift = shift % CZ
        return v if shift == 0 else pltpu.roll(v, shift, 1)

    def pack():
        packed = jnp.zeros((CZ, CZ), F32)
        for f in range(7):
            rolled = pltpu.roll(own[f].reshape(CZ, CZ), W + 8 * f, 1)
            packed = jnp.where(lane // 8 == f, rolled, packed)
        packed = packed.T
        rows = [packed[8 * f : 8 * f + 8] for f in range(7)]
        for f in range(7):
            pz[f] = rows[f]

        def quarters(group, top):
            out = turn(group[0], -12 if top else 0)
            for j in range(1, len(group)):
                out = jnp.where(slot == j, turn(group[j], 4 * j - (12 if top else 0)), out)
            return out

        halves = []
        for top in (0, 1):
            tiles = []
            for j in range(4):
                if j == 3:
                    tile = turn(rows[3], 64 * top)
                elif top:
                    tile = jnp.where(lane8 < 64, turn(rows[j], 64), rows[j + 4])
                else:
                    tile = jnp.where(lane8 < 64, rows[j], turn(rows[j + 4], 64))
                px[top, j] = tile
                tiles.append(tile)
            halves.append(tiles)
        for top in (0, 1):
            py[top, 0] = quarters(rows[0:4], top)
            py[top, 1] = quarters(rows[4:7], top)
            for xt in (0, 1):
                pc[xt, top] = quarters(halves[xt], top)

    run("pack", pack)

    beside = jnp.where(gx > 0, 9, 0) + jnp.where(gx < N - 1, 9, 0)
    pl.semaphore_wait(barrier, len(greeted) + beside)
    for k in range(1, N):
        pl.semaphore_signal(plane, inc=1, device_id=near(0, k, 0), device_id_type=MESH)

    def span(d, width, size):
        if d == 0:
            return pl.ds(0, size), pl.ds(W, size)
        if d > 0:
            return pl.ds(size - width, width), pl.ds(W - width, width)
        return pl.ds(0, width), pl.ds(W + size, width)

    halo = []

    def send(src, dst, d):
        i = len(halo)
        copy = pltpu.make_async_remote_copy(
            src_ref=src,
            dst_ref=dst,
            send_sem=hsend.at[i],
            recv_sem=hrecv.at[i],
            device_id=near(*d),
            device_id_type=MESH,
        )
        if d[0]:
            pl.when(has(d[0]))(copy.start)
        else:
            copy.start()
        halo.append((copy, d[0]))

    def received(copies):
        for copy, d in copies:
            if d:
                pl.when(has(-d))(copy.wait_recv)
            else:
                copy.wait_recv()

    for dz in (1, -1):
        part = pl.ds(0, W) if dz > 0 else pl.ds(W, W)
        send(pz.at[:, part], qz.at[:, part], (0, 0, dz))
        for d in (1, -1):
            mine, theirs = (1, 0) if d > 0 else (0, 1)
            send(px.at[mine, :, part], qx.at[theirs, :, part], (d, 0, dz))
            send(py.at[mine, :, part], qy.at[theirs, :, part], (0, d, dz))
            for dy in (1, -1):
                mine_y, theirs_y = (1, 0) if dy > 0 else (0, 1)
                send(pc.at[mine, mine_y, part], qc.at[theirs, theirs_y, part], (d, dy, dz))
    n_z = len(halo)
    flat = [(0, 1), (0, -1), (1, 0), (-1, 0), (1, 1), (1, -1), (-1, 1), (-1, -1)]
    for dx, dy in flat:
        sx4, tx4 = span(dx, W, CX)
        sy4, ty4 = span(dy, W, CY)
        sx3, tx3 = span(dx, W - 1, CX)
        sy3, ty3 = span(dy, W - 1, CY)
        if dx and dy:
            for near_x, near_y in ((2, W), (W, 2)):
                skip = 2 if near_x == W else 0
                xs = pl.ds(CX - near_x, near_x - skip) if dx > 0 else pl.ds(skip, near_x - skip)
                xt = pl.ds(W - near_x, near_x - skip) if dx > 0 else pl.ds(W + CX + skip, near_x - skip)
                ys, yt = span(dy, near_y, CY)
                send(own.at[0:3, xs, ys], a.at[:, xt, yt], (dx, dy, 0))
            send(own.at[3:6, sx3, sy3], b.at[:, tx3, ty3], (dx, dy, 0))
            send(own.at[6, sx3, sy3], c.at[tx3, ty3], (dx, dy, 0))
            continue
        send(own.at[0:3, sx4, sy4], a.at[:, tx4, ty4], (dx, dy, 0))
        send(own.at[3:6, sx3, sy3], b.at[:, tx3, ty3], (dx, dy, 0))
        send(own.at[6, sx3, sy3], c.at[tx3, ty3], (dx, dy, 0))

    for copy in local[3:]:
        copy.wait()
    def ports():
        route = iport[1]
        at64 = lax.broadcasted_iota(jnp.int32, (64, PORTS), 0) == route
        earlier = lax.broadcasted_iota(jnp.int32, (PORTS, PORTS), 0) < lax.broadcasted_iota(
            jnp.int32, (PORTS, PORTS), 1
        )
        count = dot_nn(
            jnp.where(at64, 1.0, 0.0).astype(BF16), jnp.where(earlier, 1.0, 0.0).astype(BF16)
        )
        rank = jnp.sum(jnp.where(at64, count, 0.0), axis=0, keepdims=True).astype(jnp.int32)
        slot_lane = route + 64 * (rank % 2)
        slot_row = rank // 2
        iota128 = lax.broadcasted_iota(jnp.int32, (CZ, PORTS), 0)
        lanem[...] = jnp.where(iota128 == slot_lane, 1.0, 0.0).astype(BF16)
        in_row = iota8 % 4 == slot_row
        rowm[...] = jnp.where(in_row, 1.0, 0.0)
        values = [fport[0], fport[1], fport[2], fport[3], iport[2].astype(F32) + 1.0]
        stacked = jnp.concatenate(
            [
                jnp.where(in_row, jnp.where(iota8 < 4, values[2 * i], values[min(2 * i + 1, 4)]), 0.0)
                for i in range(3)
            ],
            axis=0,
        )
        slots = three(dot_nt, stacked, lanem[...])
        for i in range(NPAR):
            ownpar[i] = slots[4 * i : 4 * i + 4]
        cell = iport[0]
        cellm[...] = jnp.where(iota128 == cell // CZ, 1.0, 0.0).astype(BF16)
        zm[...] = jnp.where(iota128 == cell % CZ, 1.0, 0.0).astype(BF16)

    run("ports", ports)

    half = pl.ds(4 * lax.rem(gy, 2), 4)
    spread_y = []
    for k in range(1, N):
        copy = pltpu.make_async_remote_copy(
            src_ref=ownpar,
            dst_ref=par.at[gz, gy // 2, :, half],
            send_sem=ysend.at[k - 1],
            recv_sem=yrecv.at[k - 1],
            device_id=(gx, lax.rem(gy + k, N), gz),
            device_id_type=MESH,
        )
        copy.start()
        spread_y.append(copy)
    own_par = pltpu.make_async_copy(ownpar, par.at[gz, gy // 2, :, half], lsem.at[0])
    own_par.start()

    received(halo[:n_z])
    low_ok = jnp.where(gz > 0, 1, 0)
    high_ok = jnp.where(gz < N - 1, 1, 0)
    keep = jnp.where(lane < CZ // 2, high_ok, low_ok) == 1

    def unpack(tiles, store):
        block = jnp.concatenate(tiles + [jnp.zeros((CZ - 56, CZ), F32)], axis=0).T
        for f in range(7):
            value = jnp.where(keep, pltpu.roll(block, (CZ - 8 * f - W) % CZ, 1), 0.0)
            ref = (ah, bh, ch)[f // 3]
            store(ref if f == 6 else ref.at[f % 3], value)

    def store_own(ref, value):
        ref[W : W + CX, W : W + CY] = value.reshape(CX, CY, CZ)

    def store_x(ref, value):
        value = value.reshape(CX, CY, CZ)
        ref[0:W, W : W + CY] = value[:W]
        ref[W + CX :, W : W + CY] = value[W:]

    def store_y(ref, value):
        value = value.reshape(CX, 4, W, CZ)
        ref[W : W + CX, 0:W] = value[:, 0]
        ref[W : W + CX, W + CY : EY] = value[:, 1]
        ref[0:W, 0:W] = value[:W, 2]
        ref[W + CX :, 0:W] = value[W:, 2]
        ref[0:W, W + CY : EY] = value[:W, 3]
        ref[W + CX :, W + CY : EY] = value[W:, 3]

    def unpack_all():
        unpack([qz[f] for f in range(7)], store_own)
        tiles = []
        for f in range(7):
            h, j = f // 4, f % 4
            if h == 0:
                tiles.append(jnp.where(lane8 < 64, qx[0, j], pltpu.roll(qx[1, j], 64, 1)))
            else:
                tiles.append(jnp.where(lane8 < 64, pltpu.roll(qx[0, j], 64, 1), qx[1, j]))
        unpack(tiles, store_x)
        tiles = []
        for f in range(7):
            h, j = f // 4, f % 4
            tile = jnp.where(slot == 0, turn(qy[0, h], -4 * j), turn(qy[1, h], 4 - 4 * j))
            for s in (0, 1):
                shift = 8 + 4 * s - 4 * j - 64 * h
                corner = jnp.where(lane8 < 64, turn(qc[0, s], shift), turn(qc[1, s], shift + 64))
                tile = jnp.where(slot == 2 + s, corner, tile)
            tiles.append(tile)
        unpack(tiles, store_y)

    run("unpack", unpack_all)

    def clear(xs, ys):
        for ref in (a, ah, b, bh):
            ref[:, xs, ys] = jnp.zeros_like(ref[:, xs, ys])
        for ref in (c, ch):
            ref[xs, ys] = jnp.zeros_like(ref[xs, ys])

    def clear_y(parts):
        @pl.when(gy == 0)
        def _():
            for xs in parts:
                clear(xs, slice(0, W))

        @pl.when(gy == N - 1)
        def _():
            for xs in parts:
                clear(xs, slice(W + CY, EY))

    received(halo[n_z : n_z + 6])
    clear_y([slice(W, W + CX)])

    def early():
        substep(a, ah, b, bh, c, ch, 5, 11, False)
        substep(b, bh, a, ah, c, ch, 6, 10, False)
        substep(a, ah, b, bh, c, ch, 7, 9, False)

    run("early", early)

    own_par.wait()
    for copy in spread_y:
        copy.wait_recv()
    spread_x = []
    for k in range(1, 4):
        copy = pltpu.make_async_remote_copy(
            src_ref=par.at[gz],
            dst_ref=par.at[gz],
            send_sem=xsend.at[k - 1],
            recv_sem=xrecv.at[k - 1],
            device_id=(gx, gy, lax.rem(gz + 2 * k, N)),
            device_id_type=MESH,
        )
        copy.start()
        spread_x.append(copy)

    received(halo[n_z + 6 :])
    clear_y([slice(0, W), slice(W + CX, EX)])

    @pl.when(gx == 0)
    def _():
        clear(slice(0, W), slice(0, EY))

    @pl.when(gx == N - 1)
    def _():
        clear(slice(W + CX, EX), slice(0, EY))

    def late():
        substep(a, ah, b, bh, c, ch, 1, 5, False)
        substep(a, ah, b, bh, c, ch, 11, 15, False)
        substep(b, bh, a, ah, c, ch, 2, 6, False)
        substep(b, bh, a, ah, c, ch, 10, 14, False)
        substep(a, ah, b, bh, c, ch, 3, 7, False)
        substep(a, ah, b, bh, c, ch, 9, 13, False)

    run("late", late)
    out_last = pltpu.make_async_copy(b.at[:, inner[0], inner[1]], last_ref, lsem.at[1])
    out_last.start()
    run("lastz", lambda: last_z(b, bh, a, c))

    def take():
        ez = a[2, W : W + CX, W : W + CY].reshape(CZ, CZ)
        picked = three(dot_nn, ez.T, cellm[...])
        sample = jnp.sum(picked * zm[...].astype(F32), axis=0, keepdims=True)
        found = three(dot_nt, rowm[...] * sample, lanem[...])
        sample8[...] = found
        ownsam[...] = found[0:4]

    run("take", take)
    pl.semaphore_wait(plane, N - 1)
    hops = lambda ky, kz: min(ky, N - ky) + min(kz, N - kz) / 2
    others = [(ky, kz) for ky in range(N) for kz in range(N) if ky or kz]
    for ky, kz in sorted(others, key=lambda k: -hops(*k)):
        pltpu.make_async_remote_copy(
            src_ref=ownsam,
            dst_ref=sam.at[gz, gy // 2, half],
            send_sem=ssend,
            recv_sem=srecv,
            device_id=near(0, ky, kz),
            device_id_type=MESH,
        ).start()
    own_sam = pltpu.make_async_copy(ownsam, sam.at[gz, gy // 2, half], lsem.at[0])
    own_sam.start()

    run("step4", lambda: substep(b, bh, a, ah, c, ch, 4, EX - 4, True))
    out_next = pltpu.make_async_copy(
        a.at[0:2, inner[0], inner[1]], next_ref.at[0:2], lsem.at[2]
    )
    out_next.start()

    for copy in spread_x:
        copy.wait_recv()
    core = lax.rem(gz, 2)
    twins = []
    for i in range(4):
        copy = pltpu.make_async_remote_copy(
            src_ref=par.at[2 * i + core],
            dst_ref=par.at[2 * i + core],
            send_sem=tsem.at[0, i],
            recv_sem=tsem.at[1, i],
            device_id=(gx, gy, gz + 1 - 2 * core),
            device_id_type=MESH,
        )
        copy.start()
        twins.append(copy)
    for copy in twins:
        copy.wait_recv()
    own_sam.wait()
    pltpu.make_async_copy(drain, drain, srecv).wait()

    def solve():
        sub = lax.broadcasted_iota(jnp.int32, (8, CZ), 0)

        def totals(first):
            def add(i, acc):
                for j in range(N // 2):
                    volt = sam[i, j] if first else node[i, j]
                    s = jnp.tanh(volt)
                    grp = par[i, j, 4]
                    acc = tuple(
                        acc[g] + jnp.where(grp == float(g + 1), s, 0.0) for g in range(GROUPS)
                    )
                return acc

            acc = lax.fori_loop(0, N, add, tuple(jnp.zeros((8, CZ), F32) for _ in range(GROUPS)))
            total = jnp.zeros((8, CZ), F32)
            for g in range(GROUPS):
                total = jnp.where(sub == g, jnp.sum(acc[g], axis=0, keepdims=True), total)
            return total + pltpu.roll(total, 64, 1)

        def newton(volt, sample, gain, drive, bias, couple, grp, total):
            s = jnp.tanh(volt)
            which = jnp.maximum(grp.astype(jnp.int32) - 1, 0)
            shared = jnp.take_along_axis(total, which, axis=0, mode="promise_in_bounds")
            resid = (1.0 + gain) * volt - sample - bias + drive * s + couple * shared
            slope = 1.0 + gain + (drive + couple) * (1.0 - s * s)
            return volt - resid / slope

        mine = sample8[...]
        my = [ownpar[i] for i in range(NPAR)]
        my = [jnp.concatenate([v, v], axis=0) for v in my]
        volt = mine
        for iterate in range(3):
            total = totals(iterate == 0)
            volt = newton(volt, mine, *my, total)
            if iterate < 2:

                def move(i, _):
                    for j in range(N // 2):
                        start = sam[i, j]
                        now = start if iterate == 0 else node[i, j]
                        node[i, j] = newton(
                            now, start, *[par[i, j, p] for p in range(NPAR)], total
                        )
                    return 0

                lax.fori_loop(0, N, move, 0)
        current8[...] = my[0] * (volt - mine)

    run("solve", solve)

    def back():
        spread = three(dot_nn, current8[...], lanem[...])
        port = jnp.sum(jnp.where(iota8 < 4, rowm[...] * spread, 0.0), axis=0, keepdims=True)
        cur_ref[...] = port
        extra = three(dot_nt, cellm[...].astype(F32) * port, zm[...])
        next_ref[2] = (a[2, W : W + CX, W : W + CY].reshape(CZ, CZ) + extra).reshape(CX, CY, CZ)

    run("back", back)
    for copy in (out_last, out_next):
        copy.wait()
    for copy, d in halo:
        if d:
            pl.when(has(d))(copy.wait_send)
        else:
            copy.wait_send()
    for copy in spread_y + spread_x + twins:
        copy.wait_send()
    pltpu.make_async_copy(drain, drain, ssend).wait()


def put_out(e_ref, last_ref, cur_ref, e_out, last_out, cur_out, sem):
    pairs = ((e_ref, e_out), (last_ref, last_out), (cur_ref, cur_out))
    copies = [pltpu.make_async_copy(s, d, sem.at[i]) for i, (s, d) in enumerate(pairs)]
    for copy in copies:
        copy.start()
    for copy in copies:
        copy.wait()


def on_device(e, ep, co, cell, route, group, gain, drive, bias, couple):
    line = lambda v: v.reshape(1, PORTS)
    any_spec = pl.BlockSpec(memory_space=pl.ANY)
    dma = pltpu.SemaphoreType.DMA
    ext, ext1 = pltpu.VMEM((3, EX, EY + 8, CZ), F32), pltpu.VMEM((EX, EY + 8, CZ), F32)
    electric, last, current = pl.pallas_call(
        kernel,
        out_shape=(
            pltpu.VMEM((3, CX, CY, CZ), F32),
            pltpu.VMEM((3, CX, CY, CZ), F32),
            pltpu.VMEM((1, PORTS), F32),
        ),
        in_specs=[any_spec] * 10,
        out_specs=(pl.BlockSpec(memory_space=pltpu.VMEM),) * 3,
        scratch_shapes=[
            pltpu.VMEM((7, CX, CY, CZ), F32),
            ext,
            ext,
            ext,
            ext,
            ext1,
            ext1,
            pltpu.VMEM((7, 8, CZ), F32),
            pltpu.VMEM((2, 4, 8, CZ), F32),
            pltpu.VMEM((2, 2, 8, CZ), F32),
            pltpu.VMEM((2, 2, 8, CZ), F32),
            pltpu.VMEM((7, 8, CZ), F32),
            pltpu.VMEM((2, 4, 8, CZ), F32),
            pltpu.VMEM((2, 2, 8, CZ), F32),
            pltpu.VMEM((2, 2, 8, CZ), F32),
            pltpu.VMEM((3, 1, PORTS), jnp.int32),
            pltpu.VMEM((4, 1, PORTS), F32),
            pltpu.VMEM((NPAR, 4, CZ), F32),
            pltpu.VMEM((4, CZ), F32),
            pltpu.VMEM((N, N // 2, NPAR, 8, CZ), F32),
            pltpu.VMEM((N, N // 2, 8, CZ), F32),
            pltpu.VMEM((N, N // 2, 8, CZ), F32),
            pltpu.VMEM((N * N - 1, 4, CZ), F32),
            pltpu.VMEM((8, PORTS), F32),
            pltpu.VMEM((CZ, PORTS), BF16),
            pltpu.VMEM((CZ, PORTS), BF16),
            pltpu.VMEM((CZ, PORTS), BF16),
            pltpu.VMEM((8, CZ), F32),
            pltpu.VMEM((8, CZ), F32),
            dma((13,)),
            dma((46,)),
            dma((46,)),
            dma((N - 1,)),
            dma((N - 1,)),
            dma((3,)),
            dma((3,)),
            dma((2, 4)),
            dma,
            dma,
            pltpu.SemaphoreType.REGULAR,
        ],
        compiler_params=pltpu.CompilerParams(
            collective_id=0, has_side_effects=True, vmem_limit_bytes=56 * 1024 * 1024
        ),
    )(e, ep, co, line(cell), line(route), line(group), line(gain), line(drive), line(bias), line(couple))
    return pl.pallas_call(
        put_out,
        out_shape=(
            jax.ShapeDtypeStruct((3, CX, CY, CZ), F32),
            jax.ShapeDtypeStruct((3, CX, CY, CZ), F32),
            jax.ShapeDtypeStruct((PORTS,), F32),
        ),
        in_specs=[any_spec] * 3,
        out_specs=(any_spec,) * 3,
        scratch_shapes=[dma((3,))],
        compiler_params=pltpu.CompilerParams(vmem_limit_bytes=1024 * 1024),
    )(electric, last, current.reshape(PORTS))


def solution(mesh):
    field = P(None, "gx", "gy", "gz")
    port = P(("gx", "gy", "gz"))
    placed = (
        field,
        field,
        P("gx", "gy", "gz"),
        port,
        P(("gx", "gy", "gz"), None),
        port,
        port,
        port,
        port,
        port,
    )
    return jax.shard_map(
        on_device,
        mesh=mesh,
        in_specs=placed,
        out_specs=(field, field, port),
        check_vma=False,
    )
```
